512 devices in a mesh: rep: 8 (over x, core), seq: 64 (over z, y).
Axes of the slice: x: 4, y: 8, z: 8, core: 2. Of those that a mesh axis runs over, the one named last changes fastest.
Arguments:
- latents: bfloat16 [32, 64, 64, 1152], P('rep', 'seq'), may hold values from -6 to 6
- destination: int32 [32], P('rep'), may hold values from 0 to 7, as said below
- token_counts: int32 [32, 64], P('rep', 'seq'), may hold values from 16 to 64, as said below
- frame_counts: int32 [32, 4], P('rep'), may hold values from 1 to 32, 64 in all within a row
- gains_spatial: float32 [3, 1152], replicated
- gains_temporal: float32 [3, 1152], replicated
- qkv_spatial: bfloat16 [1152, 1728], P(None, 'seq'), may hold values from -0.1875 to 0.1875
- proj_spatial: bfloat16 [576, 1152], P(None, 'seq'), may hold values from -0.25 to 0.25
- qkv_temporal: bfloat16 [1152, 1728], P(None, 'seq'), may hold values from -0.1875 to 0.1875
- proj_temporal: bfloat16 [576, 1152], P(None, 'seq'), may hold values from -0.25 to 0.25
- cotangent: bfloat16 [32, 64, 64, 1152], P('rep', 'seq'), may hold values from -6 to 6
Outputs:
- block_out: bfloat16 [32, 64, 64, 1152], P('rep', 'seq')
- latent_grad: bfloat16 [32, 64, 64, 1152], P('rep', 'seq')
- gain_grads: float32 [2, 3, 1152], replicated
The draws below stay inside these ranges and needn't reach their ends.
Inputs may be any that keep to these rules, and one draw needn't show every extreme that they name: `destination`: every replica group receives exactly 4 bins; no replica group sends more than 1 of its bins to one replica group, and some replica group sends exactly 1 to one. `token_counts`: frame 0 of every bin has all 64 tokens valid.
All inputs are finite; a program needn't handle non-finite values.
Results may differ from the reference program's by a relative error of at most 0.035.
Values may be sent and summed in bfloat16 or wider, within the bound.
No kernel may reach another device: no remote copies, remote signals or barrier semaphores. Data moves between devices by JAX's collectives and lax.ppermute only.
A program may use at most 128 MiB of HBM per device.

```python
import math
import jax
import jax.numpy as jnp
import numpy as np
from jax import lax

D = 1152
HEADS = 8
HD = 72
FR_DEV = 4
P_SIZE = 64
VIDS = 4
FRAMES = 64
BINS = 32
CAP = 1
N_REP = 8


def draw_destination(key, part):
    key = jax.random.fold_in(key, 11)
    key_a, key_b, key_c, key_d = jax.random.split(key, 4)
    labels = jax.random.permutation(key_a, jnp.arange(N_REP, dtype=jnp.int32))
    places = jax.random.permutation(key_b, jnp.arange(N_REP, dtype=jnp.int32))
    offsets = jax.random.permutation(key_c, jnp.arange(N_REP * CAP, dtype=jnp.int32) % N_REP)[:FR_DEV]
    row_keys = jax.random.split(key_d, N_REP)
    shuffled = jax.vmap(lambda row_key: jax.random.permutation(row_key, offsets))(row_keys)
    where = (places[:, None] + shuffled) % N_REP
    return labels[where].reshape(BINS).astype(jnp.int32)


def draw_token_counts(key, part):
    key = jax.random.fold_in(key, 12)
    counts = jax.random.randint(key, (BINS, FRAMES), P_SIZE // 4, P_SIZE + 1)
    return counts.at[:, 0].set(P_SIZE).astype(jnp.int32)


def gain_rows(key, factor):
    key_a, key_b, key_c, key_d = jax.random.split(key, 4)
    query = jax.random.uniform(key_a, (D,), jnp.float32, 0.3, 0.9)
    keys = jax.random.uniform(key_b, (D,), jnp.float32, 0.3, 0.9)
    vals = jax.random.uniform(key_c, (D,), jnp.float32, 0.5, 1.5)
    boost = jnp.where(jax.random.uniform(key_d, (D,)) < 0.25, factor, 1.0)
    return jnp.stack([query * boost, keys * boost, vals]).astype(jnp.float32)


def draw_gains_spatial(key, part):
    key = jax.random.fold_in(key, 13)
    return gain_rows(key, 1.0)


def draw_gains_temporal(key, part):
    key = jax.random.fold_in(key, 14)
    return gain_rows(key, 1.0)


def shard_levels(key, extent, cuts, least, top_value):
    factor_of, own = 1.0, jax.random.fold_in(key, 6)
    for dim, shards_of in cuts:
        steps = jnp.exp(jax.random.uniform(jax.random.fold_in(own, dim), (shards_of,), jnp.float32, least / len(cuts), top_value / len(cuts)))
        factor_of = factor_of * jnp.repeat(steps, extent[dim] // shards_of).reshape([-1 if axis == dim else 1 for axis in range(len(extent))])
    return factor_of


def length_profile(amount, total, most, skew):
    loads = [(1 << 20) // math.isqrt(rank ** skew) + 1 for rank in range(2, amount + 1)]
    spare, given = total - most - (amount - 1), [1] * (amount - 1)
    while spare > 0:
        movable = [i for i in range(amount - 1) if given[i] < most]
        whole, left = sum([loads[i] for i in movable]), spare
        for i in movable:
            addition = min(most - given[i], max(1, left * loads[i] // whole), spare)
            given[i] = given[i] + addition
            spare = spare - addition
    return np.array([most] + given)


def uneven_parts(own_key, count, total, most, skew):
    if count == 2:
        one = jax.random.randint(own_key, (), max(1, total - most), min(most, total - 1) + 1)
        return jnp.stack([one, total - one])
    lengths = jnp.asarray(length_profile(count, total, most, skew), jnp.int32)
    twos = (count - 1) // 2
    donor, taker = lengths[1:1 + 2 * twos:2], lengths[2:2 + 2 * twos:2]
    margin = jnp.minimum(donor - 1, most - taker)
    passed = jax.random.randint(jax.random.fold_in(own_key, 1), (twos,), 0, 1 << 20) % (margin + 1)
    lengths = lengths.at[1:1 + 2 * twos:2].set(donor - passed).at[2:2 + 2 * twos:2].set(taker + passed)
    return lengths[jax.random.permutation(jax.random.fold_in(own_key, 2), count)]


def scatter_about(rng, dims, scale, reach, cuts=(), held_as=jnp.bfloat16):
    entries = scale * jax.random.normal(rng, dims, jnp.float32)
    if cuts:
        entries = entries * shard_levels(rng, dims, cuts, -0.22, 0.18)
    return jnp.clip(entries, -reach, reach).astype(held_as)


def setup_inputs(seed: int = 0) -> dict:
    arg_keys = jax.random.split(jax.random.key(seed), 12)
    return {
        "latents": scatter_about(arg_keys[0], (BINS, FRAMES, P_SIZE, D), 1.0, 6.0, ((0, 8), (1, 64))),
        "destination": draw_destination(jax.random.fold_in(arg_keys[11], 71), 0),
        "token_counts": draw_token_counts(jax.random.fold_in(arg_keys[11], 71), 0),
        "frame_counts": jax.vmap(lambda own: uneven_parts(own, VIDS, FRAMES, FRAMES // 2, 2))(jax.random.split(arg_keys[3], BINS)).reshape((BINS, VIDS)).astype(jnp.int32),
        "gains_spatial": draw_gains_spatial(jax.random.fold_in(arg_keys[11], 71), 0),
        "gains_temporal": draw_gains_temporal(jax.random.fold_in(arg_keys[11], 71), 0),
        "qkv_spatial": scatter_about(arg_keys[6], (D, 3 * HEADS * HD), D ** -0.5, 0.1875, ((1, 64),)),
        "proj_spatial": scatter_about(arg_keys[7], (HEADS * HD, D), (HEADS * HD) ** -0.5, 0.25, ((1, 64),)),
        "qkv_temporal": scatter_about(arg_keys[8], (D, 3 * HEADS * HD), D ** -0.5, 0.1875, ((1, 64),)),
        "proj_temporal": scatter_about(arg_keys[9], (HEADS * HD, D), (HEADS * HD) ** -0.5, 0.25, ((1, 64),)),
        "cotangent": scatter_about(arg_keys[10], (BINS, FRAMES, P_SIZE, D), 1.0, 6.0, ((0, 8), (1, 64))),
    }


def normalize(values):
    wide = values.astype(jnp.float32)
    return wide * lax.rsqrt(lax.optimization_barrier(jnp.mean(wide * wide, axis=-1, keepdims=True)) + 1e-06)

def attend(values, gains, w_qkv, w_proj, allowed):
    normed = normalize(values)
    lead = values.shape[:-1]
    inner = HEADS * HD

    def project(which):
        scaled = (normed * gains[which]).astype(jnp.bfloat16)
        block = w_qkv[:, which * inner:(which + 1) * inner]
        made = jnp.dot(scaled, block, preferred_element_type=jnp.float32).astype(jnp.bfloat16)
        return made.reshape(lead + (HEADS, HD))
    query = project(0)
    keys = project(1)
    vals = project(2)
    scores = jnp.einsum('...qhd,...khd->...hqk', query.astype(jnp.float32), keys.astype(jnp.float32)) / math.sqrt(HD)
    scores = jnp.where(allowed, scores, -1000000000.0)
    top = lax.optimization_barrier(jnp.max(scores, axis=-1, keepdims=True))
    expo = jnp.exp(scores - top)
    weights = (expo / lax.optimization_barrier(jnp.sum(expo, axis=-1, keepdims=True))).astype(jnp.bfloat16)
    mixed = jnp.einsum('...hqk,...khd->...qhd', weights.astype(jnp.float32), vals.astype(jnp.float32))
    mixed = mixed.astype(jnp.bfloat16).reshape(lead + (inner,))
    outcome = values.astype(jnp.float32) + jnp.dot(mixed, w_proj, preferred_element_type=jnp.float32)
    return outcome.astype(jnp.bfloat16)

def one_bin(latent_bin, cot_bin, counts_bin, videos_bin, gains_spatial, gains_temporal, qkv_spatial, proj_spatial, qkv_temporal, proj_temporal):
    key_ok = jnp.arange(P_SIZE, dtype=jnp.int32)[None, :] < counts_bin[:, None]
    allowed_s = key_ok[:, None, None, :]
    ends = jnp.cumsum(videos_bin)
    video_id = lax.optimization_barrier(jnp.sum((ends[None, :] <= jnp.arange(FRAMES, dtype=jnp.int32)[:, None]).astype(jnp.int32), axis=1))
    allowed_t = (video_id[:, None] == video_id[None, :])[None, None]

    def forward(values, g_s, g_t):
        mid = attend(values, g_s, qkv_spatial, proj_spatial, allowed_s)
        out_t = attend(jnp.swapaxes(mid, 0, 1), g_t, qkv_temporal, proj_temporal, allowed_t)
        return jnp.swapaxes(out_t, 0, 1)
    out, pull = jax.vjp(forward, latent_bin, gains_spatial, gains_temporal)
    grad_in, grad_s, grad_t = pull(cot_bin)
    return (out, grad_in, grad_s, grad_t)

def reference(latents, destination, token_counts, frame_counts, gains_spatial, gains_temporal, qkv_spatial, proj_spatial, qkv_temporal, proj_temporal, cotangent):
    index = jnp.arange(BINS, dtype=jnp.int32)
    order = jnp.argsort(destination * BINS + index).astype(jnp.int32)
    inverse = jnp.argsort(order).astype(jnp.int32)
    moved = latents[order]

    def step(item):
        return one_bin(item[0], item[1], item[2], item[3], gains_spatial, gains_temporal, qkv_spatial, proj_spatial, qkv_temporal, proj_temporal)
    outs, grads, grad_s, grad_t = lax.map(step, (moved, cotangent, token_counts, frame_counts))
    gain_grads = jnp.stack([lax.optimization_barrier(jnp.sum(grad_s, axis=0)), lax.optimization_barrier(jnp.sum(grad_t, axis=0))])
    return (outs, grads[inverse], gain_grads)
```

```python
import math

import jax
import jax.numpy as jnp
from jax import lax
from jax.sharding import Mesh
from jax.sharding import PartitionSpec as P

HEADS = 8
HD = 72
INNER = HEADS * HD
SEQ = ("z", "y")
W_PAD = 1792
U_CUT = 640


def normalize(values):
    wide = values.astype(jnp.float32)
    return wide * lax.rsqrt(jnp.mean(wide * wide, axis=-1, keepdims=True) + 1e-06)


def attend(values, gains, w_qkv, w_proj, allowed):
    normed = normalize(values)
    lead = values.shape[:-1]

    def project(which):
        scaled = (normed * gains[which]).astype(jnp.bfloat16)
        block = w_qkv[:, which * INNER : (which + 1) * INNER]
        made = jnp.dot(scaled, block, preferred_element_type=jnp.float32).astype(jnp.bfloat16)
        return made.reshape(lead + (HEADS, HD))

    query = project(0)
    keys = project(1)
    vals = project(2)
    scores = jnp.einsum(
        "...qhd,...khd->...hqk", query, keys, preferred_element_type=jnp.float32
    ) / math.sqrt(HD)
    scores = jnp.where(allowed, scores, -1000000000.0)
    top = jnp.max(scores, axis=-1, keepdims=True)
    expo = jnp.exp(scores - top)
    weights = (expo / jnp.sum(expo, axis=-1, keepdims=True)).astype(jnp.bfloat16)
    mixed = jnp.einsum("...hqk,...khd->...qhd", weights, vals, preferred_element_type=jnp.float32)
    mixed = mixed.astype(jnp.bfloat16).reshape(lead + (INNER,))
    outcome = values.astype(jnp.float32) + jnp.dot(
        mixed, w_proj, preferred_element_type=jnp.float32
    )
    return outcome.astype(jnp.bfloat16)


def exchange(rows, axes):
    return lax.all_to_all(rows, axes, split_axis=0, concat_axis=0, tiled=True)


def spread(value, axes):
    peers = lax.axis_size(axes)
    return exchange(jnp.broadcast_to(value[None], (peers,) + value.shape), axes)


def gather_weights(qkv, proj):
    rep = lax.axis_index("rep")
    groups = lax.axis_size("rep")
    depth, shard = qkv.shape
    inner, shard_u = proj.shape
    rows_w, rows_u = depth // groups, inner // groups
    piece_w = lax.dynamic_slice(qkv.T, (0, rep * rows_w), (shard, rows_w)).reshape(-1)
    piece_u = lax.dynamic_slice(proj.T, (0, rep * rows_u), (shard_u, rows_u)).reshape(-1)
    flat = jnp.concatenate([piece_w, piece_u])
    flat = jnp.pad(flat, (0, -flat.shape[0] % 128))
    got = spread(flat, SEQ)
    peers = got.shape[0]
    part_w = got[:, : shard * rows_w].reshape(peers * shard, rows_w).T
    part_u = got[:, shard * rows_w : shard * rows_w + shard_u * rows_u]
    part_u = part_u.reshape(peers * shard_u, rows_u).T
    part_w = jnp.pad(part_w, ((0, 0), (0, W_PAD - part_w.shape[1])))
    low, high = part_u[:, :U_CUT], part_u[:, U_CUT:]
    high = jnp.pad(high, ((0, 0), (0, U_CUT - high.shape[1])))
    part = jnp.concatenate([part_w, jnp.concatenate([low, high], axis=0)], axis=1)
    return lax.all_gather(part, "rep", axis=0, tiled=False)


def unpack_weights(full, depth, inner):
    rows_u = inner // full.shape[0]
    w_qkv = full[:, :, : 3 * inner].reshape(depth, 3 * inner)
    low = full[:, :rows_u, W_PAD : W_PAD + U_CUT]
    high = full[:, rows_u : 2 * rows_u, W_PAD : W_PAD + depth - U_CUT]
    w_proj = jnp.concatenate([low, high], axis=2).reshape(inner, depth)
    return w_qkv, w_proj


def local(
    latents,
    destination,
    token_counts,
    frame_counts,
    gains_spatial,
    gains_temporal,
    qkv_spatial,
    proj_spatial,
    qkv_temporal,
    proj_temporal,
    cotangent,
):
    bins_here, _, slots, width = latents.shape
    groups = lax.axis_size("rep")
    frames = lax.axis_size(SEQ)
    group = lax.axis_index("rep")
    place = lax.axis_index(SEQ)
    inner = proj_spatial.shape[0]
    tokens = bins_here * slots // frames

    full_s = gather_weights(qkv_spatial, proj_spatial)

    mine = jnp.concatenate([destination, token_counts[:, 0], frame_counts.reshape(-1)])
    mine = jnp.pad(mine, (0, 128 - mine.shape[0]))
    facts = spread(mine[None], "rep")[:, 0]
    dest_all = facts[:, :bins_here]
    tokens_all = facts[:, bins_here : 2 * bins_here].reshape(-1)
    videos_all = facts[:, 2 * bins_here : 2 * bins_here + frame_counts.size]
    videos_all = videos_all.reshape(groups * bins_here, -1)
    earlier = (dest_all[None] == destination[:, None, None]) & (
        jnp.arange(groups, dtype=jnp.int32)[None, :, None] < group
    )
    new_place = destination * bins_here + jnp.sum(earlier.astype(jnp.int32), axis=(1, 2))
    pick_new = (new_place[:, None] == jnp.arange(groups * bins_here, dtype=jnp.int32)).astype(
        jnp.int32
    )
    my_tokens = jnp.sum(pick_new * tokens_all[None], axis=1)
    my_videos = jnp.sum(pick_new[:, :, None] * videos_all[None], axis=1)
    comes = jnp.any(dest_all == group, axis=1).astype(jnp.int32)
    rank_of = jnp.clip(jnp.cumsum(comes) - 1, 0, bins_here - 1)
    group_ids = jnp.arange(groups, dtype=jnp.int32)
    bin_ids = jnp.arange(bins_here, dtype=jnp.int32)
    from_group = jnp.sum(
        ((rank_of[None] == bin_ids[:, None]) & (comes[None] > 0)).astype(jnp.int32)
        * group_ids[None],
        axis=1,
    )
    bin_to = jnp.sum(
        (destination[None] == group_ids[:, None]).astype(jnp.int32) * bin_ids[None], axis=1
    )

    cot_sent = cotangent[:, 0][rank_of]
    cot_here = exchange(cot_sent, "rep")[destination]
    cot_tokens = exchange(cot_here.reshape(frames, tokens, width), SEQ)
    full_t = gather_weights(qkv_temporal, proj_temporal)

    key_ok = jnp.arange(slots, dtype=jnp.int32)[None, :] < my_tokens[:, None]
    allowed_s = key_ok[:, None, None, None, :]
    ends = jnp.cumsum(my_videos, axis=1)
    video_id = jnp.sum(
        (ends[:, None, :] <= jnp.arange(frames, dtype=jnp.int32)[None, :, None]).astype(jnp.int32),
        axis=2,
    )
    row_bin = place * tokens // slots
    video_row = jnp.sum((bin_ids == row_bin).astype(jnp.int32)[:, None] * video_id, axis=0)
    allowed_t = (video_row[:, None] == video_row[None, :])[None, None]

    w_s, u_s = unpack_weights(full_s, width, inner)
    mid, pull_spatial = jax.vjp(
        lambda v, g: attend(v, g, w_s, u_s, allowed_s), latents, gains_spatial
    )
    mid_tokens = exchange(mid.reshape(frames, tokens, width), SEQ)
    w_t, u_t = unpack_weights(full_t, width, inner)
    out_tokens, pull_temporal = jax.vjp(
        lambda v, g: attend(v, g, w_t, u_t, allowed_t),
        jnp.swapaxes(mid_tokens, 0, 1),
        gains_temporal,
    )
    mid_grad_tokens, grad_temporal = pull_temporal(jnp.swapaxes(cot_tokens, 0, 1))
    both = jnp.concatenate([mid_grad_tokens, out_tokens], axis=0)
    both = exchange(jnp.swapaxes(both, 0, 1), SEQ)
    mid_grad = both[:, :tokens].reshape(bins_here, 1, slots, width)
    out_here = both[:, tokens:].reshape(bins_here, slots, width)
    block_out = exchange(out_here[bin_to], "rep")[from_group]
    latent_grad, grad_spatial = pull_spatial(mid_grad)
    sums = jnp.stack([grad_spatial, grad_temporal]).reshape(8, -1)
    for axis in ("y", "z", "rep"):
        sums = jnp.sum(spread(sums, axis), axis=0)
    gain_grads = sums.reshape((2,) + gains_spatial.shape)
    return (block_out[:, None], latent_grad, gain_grads)


def solution(mesh):
    rep, seq = mesh.devices.shape
    deep = Mesh(mesh.devices.reshape(rep, 8, seq // 8), ("rep", "z", "y"))
    in_specs = (
        P("rep", SEQ, None, None),
        P("rep"),
        P("rep", SEQ),
        P("rep", None),
        P(),
        P(),
        P(None, SEQ),
        P(None, SEQ),
        P(None, SEQ),
        P(None, SEQ),
        P("rep", SEQ, None, None),
    )
    out_specs = (P("rep", SEQ, None, None), P("rep", SEQ, None, None), P())
    return jax.shard_map(local, mesh=deep, in_specs=in_specs, out_specs=out_specs, check_vma=False)
```

```python
import math

import jax
import jax.numpy as jnp
from jax import lax
from jax.experimental import pallas as pl
from jax.experimental.pallas import tpu as pltpu
from jax.sharding import Mesh
from jax.sharding import PartitionSpec as P

HEADS = 8
HD = 72
INNER = HEADS * HD
SEQ = ("z", "y")
W_PAD = 1792
U_CUT = 640


def scores_of(q_ref, k_ref, head, allowed):
    rows = slice(HD * head, HD * head + HD)
    query = q_ref[rows, :].astype(jnp.bfloat16)
    keys = k_ref[rows, :].astype(jnp.bfloat16)
    raw = lax.dot_general(
        keys, query, (((0,), (0,)), ((), ())), preferred_element_type=jnp.float32
    )
    raw = jnp.where(allowed, raw * (1.0 / math.sqrt(HD)), -1000000000.0)
    expo = jnp.exp(raw - jnp.max(raw, axis=0, keepdims=True))
    weights = expo * (1.0 / jnp.sum(expo, axis=0, keepdims=True))
    return query, keys, weights


def normed_of(v_ref):
    wide = v_ref[...].astype(jnp.float32)
    scale = lax.rsqrt(jnp.mean(wide * wide, axis=1, keepdims=True) + 1e-06)
    return wide * scale, scale


def load_u(full_ref, u_ref):
    for part in range(8):
        block = full_ref[144 * part : 144 * part + 144, W_PAD : W_PAD + U_CUT].astype(jnp.float32)
        u_ref[72 * part : 72 * part + 72, :U_CUT] = block[:72]
        u_ref[72 * part : 72 * part + 72, U_CUT:] = block[72:, : 1152 - U_CUT]


def forward(v_ref, gains_ref, full_ref, key_label, query_label, out_ref, q_ref, k_ref, x_ref, o_ref, u_ref):
    normed, scale = normed_of(v_ref)

    def project(which, first, past):
        scaled = (normed * gains_ref[which : which + 1, :]).astype(jnp.bfloat16)
        made = jnp.dot(scaled, full_ref[:, first:past], preferred_element_type=jnp.float32)
        return jnp.transpose(made)

    q_ref[...] = project(0, 0, 640)[:INNER]
    k_ref[...] = project(1, 512, 1152)[64:]
    x_ref[...] = project(2, 1152, 1792)[:INNER]
    allowed = key_label == query_label
    for head in range(HEADS):
        rows = slice(HD * head, HD * head + HD)
        _, _, weights = scores_of(q_ref, k_ref, head, allowed)
        vals = x_ref[rows, :].astype(jnp.bfloat16)
        o_ref[rows, :] = jnp.dot(
            vals, weights.astype(jnp.bfloat16), preferred_element_type=jnp.float32
        )
    mixed = jnp.transpose(o_ref[...]).astype(jnp.bfloat16)
    made = jnp.dot(mixed, u_ref[...].astype(jnp.bfloat16), preferred_element_type=jnp.float32)
    out_ref[...] = (v_ref[...].astype(jnp.float32) + made).astype(jnp.bfloat16)


def backward(
    g_ref, v_ref, gains_ref, full_ref, key_label, query_label, grad_ref, gain_ref,
    q_ref, k_ref, x_ref, o_ref, u_ref, dq_ref, dk_ref, dx_ref,
):
    grad = g_ref[...]
    o_ref[...] = lax.dot_general(
        u_ref[...].astype(jnp.bfloat16),
        grad,
        (((1,), (1,)), ((), ())),
        preferred_element_type=jnp.float32,
    )
    zeros = jnp.zeros((640 - INNER, dq_ref.shape[1]), jnp.float32)
    dq_ref[INNER:, :] = zeros
    dk_ref[: 640 - INNER, :] = zeros
    dx_ref[INNER:, :] = zeros
    allowed = key_label == query_label
    over_lanes = (((1,), (1,)), ((), ()))
    for head in range(HEADS):
        low = HD * head
        rows = slice(low, low + HD)
        query, keys, weights = scores_of(q_ref, k_ref, head, allowed)
        vals = x_ref[rows, :].astype(jnp.bfloat16)
        d_out = o_ref[rows, :].astype(jnp.bfloat16)
        d_weights = lax.dot_general(
            vals, d_out, (((0,), (0,)), ((), ())), preferred_element_type=jnp.float32
        )
        along = jnp.sum(d_weights * weights, axis=0, keepdims=True)
        d_scores = weights * (d_weights - along) * (1.0 / math.sqrt(HD))
        d_scores = d_scores.astype(jnp.bfloat16)
        dq_ref[rows, :] = jnp.dot(keys, d_scores, preferred_element_type=jnp.float32)
        dk_ref[64 + low : 64 + low + HD, :] = lax.dot_general(
            query, d_scores, over_lanes, preferred_element_type=jnp.float32
        )
        dx_ref[rows, :] = lax.dot_general(
            d_out, weights.astype(jnp.bfloat16), over_lanes, preferred_element_type=jnp.float32
        )
    normed, scale = normed_of(v_ref)
    d_normed = None
    for which, (ref, first) in enumerate(((dq_ref, 0), (dk_ref, 512), (dx_ref, 1152))):
        made = jnp.transpose(ref[...]).astype(jnp.bfloat16)
        back = lax.dot_general(
            made, full_ref[:, first : first + 640], over_lanes, preferred_element_type=jnp.float32
        )
        gain_ref[which : which + 1, :] = jnp.sum(back * normed, axis=0, keepdims=True)
        term = back * gains_ref[which : which + 1, :]
        d_normed = term if d_normed is None else d_normed + term
    inward = jnp.mean(d_normed * normed, axis=1, keepdims=True)
    result = grad.astype(jnp.float32) + scale * (d_normed - normed * inward)
    grad_ref[...] = result.astype(jnp.bfloat16)


def spatial_forward_kernel(v, gains, full, lab_k, lab_q, mid, qkv, q, k, x, o, u):
    load_u(full, u)
    forward(v, gains, full, lab_k[...], lab_q[...], mid, q, k, x, o, u)
    for which, ref in enumerate((q, k, x)):
        qkv[which] = ref[...].astype(jnp.bfloat16)


def spatial_backward_kernel(
    g, v, gains, full, lab_k, lab_q, qkv, grad, gain, q, k, x, o, u, dq, dk, dx
):
    load_u(full, u)
    for which, ref in enumerate((q, k, x)):
        ref[...] = qkv[which].astype(jnp.float32)
    backward(g, v, gains, full, lab_k[...], lab_q[...], grad, gain, q, k, x, o, u, dq, dk, dx)


def temporal_kernel(
    g, v, gains, full, lab_k, lab_q, out, grad, gain, q, k, x, o, u, dq, dk, dx
):
    load_u(full, u)
    forward(v, gains, full, lab_k[...], lab_q[...], out, q, k, x, o, u)
    backward(g, v, gains, full, lab_k[...], lab_q[...], grad, gain, q, k, x, o, u, dq, dk, dx)


def call_kernel(kernel, outs, backs, name):
    rows = 256
    wide = pltpu.VMEM((INNER, rows), jnp.float32)
    scratch = [wide] * 4 + [pltpu.VMEM((INNER, 1152), jnp.float32)]
    if backs:
        scratch += [pltpu.VMEM((640, rows), jnp.float32)] * 3
    return pl.pallas_call(
        kernel,
        out_shape=outs,
        scratch_shapes=scratch,
        compiler_params=pltpu.CompilerParams(vmem_limit_bytes=50 * 1024 * 1024),
        cost_estimate=pl.CostEstimate(
            flops=int(6e9), bytes_accessed=int(8e6), transcendentals=int(5e5)
        ),
        name=name,
    )


ROWS_OUT = jax.ShapeDtypeStruct((256, 1152), jnp.bfloat16)
GAIN_OUT = jax.ShapeDtypeStruct((3, 1152), jnp.float32)
QKV_OUT = jax.ShapeDtypeStruct((3, 576, 256), jnp.bfloat16)


def exchange(rows, axes):
    return lax.all_to_all(rows, axes, split_axis=0, concat_axis=0, tiled=True)


def spread(value, axes):
    peers = lax.axis_size(axes)
    return exchange(jnp.broadcast_to(value[None], (peers,) + value.shape), axes)


def own_piece(qkv, proj, rep, groups):
    rows_w, rows_u = qkv.shape[0] // groups, proj.shape[0] // groups
    piece_w = lax.dynamic_slice(qkv.T, (0, rep * rows_w), (qkv.shape[1], rows_w)).reshape(-1)
    piece_u = lax.dynamic_slice(proj.T, (0, rep * rows_u), (proj.shape[1], rows_u)).reshape(-1)
    return jnp.concatenate([piece_w, piece_u])


def gather_weights(got, shard, shard_u, rows_w, rows_u):
    peers = got.shape[0]
    cut = shard * rows_w
    part_w = got[:, :cut].reshape(peers * shard, rows_w).T
    part_u = got[:, cut : cut + shard_u * rows_u].reshape(peers * shard_u, rows_u).T
    part_w = jnp.pad(part_w, ((0, 0), (0, W_PAD - part_w.shape[1])))
    low, high = part_u[:, :U_CUT], part_u[:, U_CUT:]
    high = jnp.pad(high, ((0, 0), (0, U_CUT - high.shape[1])))
    part = jnp.concatenate([part_w, jnp.concatenate([low, high], axis=0)], axis=1)
    full = lax.all_gather(part, "rep", axis=0, tiled=False)
    return full.reshape(full.shape[0] * full.shape[1], full.shape[2])


def local(
    latents,
    destination,
    token_counts,
    frame_counts,
    gains_spatial,
    gains_temporal,
    qkv_spatial,
    proj_spatial,
    qkv_temporal,
    proj_temporal,
    cotangent,
):
    bins_here, _, slots, width = latents.shape
    groups = lax.axis_size("rep")
    frames = lax.axis_size(SEQ)
    group = lax.axis_index("rep")
    place = lax.axis_index(SEQ)
    inner = proj_spatial.shape[0]
    tokens = bins_here * slots // frames
    rows = bins_here * slots
    sizes = (qkv_spatial.shape[1], proj_spatial.shape[1], width // groups, inner // groups)

    mine = jnp.concatenate([destination, token_counts[:, 0], frame_counts.reshape(-1)])
    mine = jnp.pad(mine.astype(jnp.bfloat16)[None], ((0, 15), (0, width - mine.shape[0])))
    sent = jnp.concatenate([cotangent.reshape(rows, width), mine], axis=0)
    shared = lax.all_gather(sent, "rep", axis=0, tiled=False)

    flat_s = own_piece(qkv_spatial, proj_spatial, group, groups)
    flat_s = jnp.pad(flat_s, (0, -flat_s.shape[0] % 256))
    got_s = spread(flat_s.reshape(2, -1), SEQ).reshape(frames, -1)
    full_s = gather_weights(got_s, *sizes)

    facts = shared[:, rows, :128].astype(jnp.int32)
    dest_all = facts[:, :bins_here]
    tokens_all = facts[:, bins_here : 2 * bins_here].reshape(-1)
    videos_all = facts[:, 2 * bins_here : 2 * bins_here + frame_counts.size]
    videos_all = videos_all.reshape(groups * bins_here, -1)
    group_ids = jnp.arange(groups, dtype=jnp.int32)
    bin_ids = jnp.arange(bins_here, dtype=jnp.int32)
    earlier = (dest_all[None] == destination[:, None, None]) & (
        group_ids[None, :, None] < group
    )
    rank = jnp.sum(earlier.astype(jnp.int32), axis=(1, 2))
    new_place = destination * bins_here + rank
    pick_new = (new_place[:, None] == jnp.arange(groups * bins_here, dtype=jnp.int32)).astype(
        jnp.int32
    )
    my_tokens = jnp.sum(pick_new * tokens_all[None], axis=1)
    my_videos = jnp.sum(pick_new[:, :, None] * videos_all[None], axis=1)
    comes = jnp.any(dest_all == group, axis=1).astype(jnp.int32)
    order = jnp.cumsum(comes) - 1
    source = ((order[None] == bin_ids[:, None]) & (comes[None] > 0)).astype(jnp.int32)
    from_group = jnp.sum(source * group_ids[None], axis=1)
    bin_there = jnp.sum((dest_all == group).astype(jnp.int32) * bin_ids[None], axis=1)
    from_bin = jnp.sum(source * bin_there[None], axis=1)

    cot_here = jnp.stack(
        [
            lax.dynamic_slice(shared, (destination[i], rank[i] * slots, 0), (1, slots, width))[0]
            for i in range(bins_here)
        ]
    )
    flat_t = own_piece(qkv_temporal, proj_temporal, group, groups).reshape(tokens, -1)
    flat_t = jnp.pad(flat_t, ((0, 0), (0, -flat_t.shape[1] % 128)))
    mixed = jnp.concatenate(
        [
            cot_here.reshape(frames, tokens, width),
            jnp.broadcast_to(flat_t[None], (frames,) + flat_t.shape),
        ],
        axis=2,
    )
    mixed = exchange(mixed, SEQ)
    cot_tokens = mixed[:, :, :width].reshape(rows, width)
    piece = sizes[0] * sizes[2] + sizes[1] * sizes[3]
    full_t = gather_weights(
        mixed[:, :, width : width + piece // tokens].reshape(frames, -1), *sizes
    )

    key_ok = jnp.arange(slots, dtype=jnp.int32)[None, :] < my_tokens[:, None]
    lab_k = jnp.where(key_ok, bin_ids[:, None], -1).reshape(rows, 1)
    lab_q = jnp.broadcast_to(bin_ids[:, None], (bins_here, slots)).reshape(1, rows)
    values = latents.reshape(rows, width)
    mid, qkv = call_kernel(spatial_forward_kernel, (ROWS_OUT, QKV_OUT), False, "spatial_forward")(
        values, gains_spatial, full_s, lab_k, lab_q
    )
    mid_tokens = exchange(mid.reshape(frames, tokens, width), SEQ).reshape(rows, width)

    ends = jnp.cumsum(my_videos, axis=1)
    video_id = jnp.sum(
        (ends[:, None, :] <= jnp.arange(frames, dtype=jnp.int32)[None, :, None]).astype(jnp.int32),
        axis=2,
    )
    row_bin = place * tokens // slots
    video_row = jnp.sum((bin_ids == row_bin).astype(jnp.int32)[:, None] * video_id, axis=0)
    lab_t = video_row[:, None] * tokens + jnp.arange(tokens, dtype=jnp.int32)[None]
    out_tokens, mid_grad_tokens, grad_temporal = call_kernel(
        temporal_kernel, (ROWS_OUT, ROWS_OUT, GAIN_OUT), True, "temporal"
    )(cot_tokens, mid_tokens, gains_temporal, full_t, lab_t.reshape(rows, 1), lab_t.reshape(1, rows))

    both = jnp.concatenate(
        [
            mid_grad_tokens.reshape(frames, tokens, width),
            out_tokens.reshape(frames, tokens, width),
        ],
        axis=1,
    )
    both = exchange(both, SEQ)
    mid_grad = both[:, :tokens].reshape(rows, width)
    outs = lax.all_gather(both[:, tokens:].reshape(rows, width), "rep", axis=0, tiled=False)
    block_out = jnp.stack(
        [
            lax.dynamic_slice(outs, (from_group[j], from_bin[j] * slots, 0), (1, slots, width))
            for j in range(bins_here)
        ]
    )
    latent_grad, grad_spatial = call_kernel(
        spatial_backward_kernel, (ROWS_OUT, GAIN_OUT), True, "spatial_backward"
    )(mid_grad, values, gains_spatial, full_s, lab_k, lab_q, qkv)
    sums = jnp.stack([grad_spatial, grad_temporal]).reshape(8, -1)
    for axis in ("y", "z", "rep"):
        sums = jnp.sum(spread(sums, axis), axis=0)
    gain_grads = sums.reshape((2,) + gains_spatial.shape)
    return (block_out, latent_grad.reshape(latents.shape), gain_grads)


def solution(mesh):
    rep, seq = mesh.devices.shape
    deep = Mesh(mesh.devices.reshape(rep, 8, seq // 8), ("rep", "z", "y"))
    in_specs = (
        P("rep", SEQ, None, None),
        P("rep"),
        P("rep", SEQ),
        P("rep", None),
        P(),
        P(),
        P(None, SEQ),
        P(None, SEQ),
        P(None, SEQ),
        P(None, SEQ),
        P("rep", SEQ, None, None),
    )
    out_specs = (P("rep", SEQ, None, None), P("rep", SEQ, None, None), P())
    return jax.shard_map(local, mesh=deep, in_specs=in_specs, out_specs=out_specs, check_vma=False)
```

```python
import math

import jax
import jax.numpy as jnp
from jax import lax
from jax.experimental import pallas as pl
from jax.experimental.pallas import tpu as pltpu
from jax.sharding import Mesh
from jax.sharding import PartitionSpec as P

HEADS = 8
HD = 72
INNER = HEADS * HD
SEQ = ("z", "y")
W_PAD = 1792
U_CUT = 640


def scores_of(q_ref, k_ref, head, allowed):
    rows = slice(HD * head, HD * head + HD)
    query = q_ref[rows, :].astype(jnp.bfloat16)
    keys = k_ref[rows, :].astype(jnp.bfloat16)
    raw = lax.dot_general(
        keys, query, (((0,), (0,)), ((), ())), preferred_element_type=jnp.float32
    )
    raw = jnp.where(allowed, raw * (1.0 / math.sqrt(HD)), -1000000000.0)
    expo = jnp.exp(raw - jnp.max(raw, axis=0, keepdims=True))
    weights = expo * (1.0 / jnp.sum(expo, axis=0, keepdims=True))
    return query, keys, weights


def normed_of(v_ref):
    wide = v_ref[...].astype(jnp.float32)
    scale = lax.rsqrt(jnp.mean(wide * wide, axis=1, keepdims=True) + 1e-06)
    return wide * scale, scale


def load_u(full_ref, u_ref):
    for part in range(8):
        block = full_ref[144 * part : 144 * part + 144, W_PAD : W_PAD + U_CUT].astype(jnp.float32)
        u_ref[72 * part : 72 * part + 72, :U_CUT] = block[:72]
        u_ref[72 * part : 72 * part + 72, U_CUT:] = block[72:, : 1152 - U_CUT]


def forward(v_ref, gains_ref, full_ref, key_label, query_label, q_ref, k_ref, x_ref, o_ref):
    normed, scale = normed_of(v_ref)

    def project(which, first, past):
        scaled = (normed * gains_ref[which : which + 1, :]).astype(jnp.bfloat16)
        made = jnp.dot(scaled, full_ref[:, first:past], preferred_element_type=jnp.float32)
        return jnp.transpose(made)

    q_ref[...] = project(0, 0, 640)[:INNER]
    k_ref[...] = project(1, 512, 1152)[64:]
    x_ref[...] = project(2, 1152, 1792)[:INNER]
    allowed = key_label == query_label
    for head in range(HEADS):
        rows = slice(HD * head, HD * head + HD)
        _, _, weights = scores_of(q_ref, k_ref, head, allowed)
        vals = x_ref[rows, :].astype(jnp.bfloat16)
        o_ref[rows, :] = jnp.dot(
            vals, weights.astype(jnp.bfloat16), preferred_element_type=jnp.float32
        )
    return jnp.transpose(o_ref[...]).astype(jnp.bfloat16)


def finish(v_ref, mixed, u_ref, out_ref):
    made = jnp.dot(mixed, u_ref[...].astype(jnp.bfloat16), preferred_element_type=jnp.float32)
    out_ref[...] = (v_ref[...].astype(jnp.float32) + made).astype(jnp.bfloat16)


def backward(
    g_ref, v_ref, gains_ref, full_ref, key_label, query_label, grad_ref, gain_ref,
    q_ref, k_ref, x_ref, o_ref, u_ref, dq_ref, dk_ref, dx_ref,
):
    grad = g_ref[...]
    o_ref[...] = lax.dot_general(
        u_ref[...].astype(jnp.bfloat16),
        grad,
        (((1,), (1,)), ((), ())),
        preferred_element_type=jnp.float32,
    )
    zeros = jnp.zeros((640 - INNER, dq_ref.shape[1]), jnp.float32)
    dq_ref[INNER:, :] = zeros
    dk_ref[: 640 - INNER, :] = zeros
    dx_ref[INNER:, :] = zeros
    allowed = key_label == query_label
    over_lanes = (((1,), (1,)), ((), ()))
    for head in range(HEADS):
        low = HD * head
        rows = slice(low, low + HD)
        query, keys, weights = scores_of(q_ref, k_ref, head, allowed)
        vals = x_ref[rows, :].astype(jnp.bfloat16)
        d_out = o_ref[rows, :].astype(jnp.bfloat16)
        d_weights = lax.dot_general(
            vals, d_out, (((0,), (0,)), ((), ())), preferred_element_type=jnp.float32
        )
        along = jnp.sum(d_weights * weights, axis=0, keepdims=True)
        d_scores = weights * (d_weights - along) * (1.0 / math.sqrt(HD))
        d_scores = d_scores.astype(jnp.bfloat16)
        dq_ref[rows, :] = jnp.dot(keys, d_scores, preferred_element_type=jnp.float32)
        dk_ref[64 + low : 64 + low + HD, :] = lax.dot_general(
            query, d_scores, over_lanes, preferred_element_type=jnp.float32
        )
        dx_ref[rows, :] = lax.dot_general(
            d_out, weights.astype(jnp.bfloat16), over_lanes, preferred_element_type=jnp.float32
        )
    normed, scale = normed_of(v_ref)
    d_normed = None
    for which, (ref, first) in enumerate(((dq_ref, 0), (dk_ref, 512), (dx_ref, 1152))):
        made = jnp.transpose(ref[...]).astype(jnp.bfloat16)
        back = lax.dot_general(
            made, full_ref[:, first : first + 640], over_lanes, preferred_element_type=jnp.float32
        )
        gain_ref[which : which + 1, :] = jnp.sum(back * normed, axis=0, keepdims=True)
        term = back * gains_ref[which : which + 1, :]
        d_normed = term if d_normed is None else d_normed + term
    inward = jnp.mean(d_normed * normed, axis=1, keepdims=True)
    result = grad.astype(jnp.float32) + scale * (d_normed - normed * inward)
    grad_ref[...] = result.astype(jnp.bfloat16)


def spatial_forward_kernel(v, gains, full, lab_k, lab_q, mid, qkv, q, k, x, o, u):
    load_u(full, u)
    finish(v, forward(v, gains, full, lab_k[...], lab_q[...], q, k, x, o), u, mid)
    for which, ref in enumerate((q, k, x)):
        qkv[which] = ref[...].astype(jnp.bfloat16)


def spatial_backward_kernel(
    g, v, gains, full, lab_k, lab_q, qkv, grad, gain, q, k, x, o, u, dq, dk, dx
):
    load_u(full, u)
    for which, ref in enumerate((q, k, x)):
        ref[...] = qkv[which].astype(jnp.float32)
    backward(g, v, gains, full, lab_k[...], lab_q[...], grad, gain, q, k, x, o, u, dq, dk, dx)


def temporal_kernel(
    g, v, gains, full, lab_k, lab_q, mixed, grad, gain, q, k, x, o, u, dq, dk, dx
):
    load_u(full, u)
    mixed[...] = forward(v, gains, full, lab_k[...], lab_q[...], q, k, x, o)
    backward(g, v, gains, full, lab_k[...], lab_q[...], grad, gain, q, k, x, o, u, dq, dk, dx)


def finish_kernel(v, mixed, full, out, u):
    load_u(full, u)
    finish(v, mixed[...], u, out)


def call_kernel(kernel, outs, backs, name):
    rows = 256
    wide = pltpu.VMEM((INNER, rows), jnp.float32)
    scratch = [wide] * 4 + [pltpu.VMEM((INNER, 1152), jnp.float32)]
    if kernel is finish_kernel:
        scratch = scratch[4:]
    if backs:
        scratch += [pltpu.VMEM((640, rows), jnp.float32)] * 3
    return pl.pallas_call(
        kernel,
        out_shape=outs,
        scratch_shapes=scratch,
        compiler_params=pltpu.CompilerParams(vmem_limit_bytes=50 * 1024 * 1024),
        cost_estimate=pl.CostEstimate(
            flops=int(6e9), bytes_accessed=int(8e6), transcendentals=int(5e5)
        ),
        name=name,
    )


ROWS_OUT = jax.ShapeDtypeStruct((256, 1152), jnp.bfloat16)
MIXED_OUT = jax.ShapeDtypeStruct((256, 576), jnp.bfloat16)
GAIN_OUT = jax.ShapeDtypeStruct((3, 1152), jnp.float32)
QKV_OUT = jax.ShapeDtypeStruct((3, 576, 256), jnp.bfloat16)


def exchange(rows, axes):
    return lax.all_to_all(rows, axes, split_axis=0, concat_axis=0, tiled=True)


def spread(value, axes):
    peers = lax.axis_size(axes)
    return exchange(jnp.broadcast_to(value[None], (peers,) + value.shape), axes)


def own_piece(qkv, proj, rep, groups):
    rows_w, rows_u = qkv.shape[0] // groups, proj.shape[0] // groups
    piece_w = lax.dynamic_slice(qkv.T, (0, rep * rows_w), (qkv.shape[1], rows_w)).reshape(-1)
    piece_u = lax.dynamic_slice(proj.T, (0, rep * rows_u), (proj.shape[1], rows_u)).reshape(-1)
    return jnp.concatenate([piece_w, piece_u])


def gather_weights(got, shard, shard_u, rows_w, rows_u):
    peers = got.shape[0]
    cut = shard * rows_w
    part_w = got[:, :cut].reshape(peers * shard, rows_w).T
    part_u = got[:, cut : cut + shard_u * rows_u].reshape(peers * shard_u, rows_u).T
    part_w = jnp.pad(part_w, ((0, 0), (0, W_PAD - part_w.shape[1])))
    low, high = part_u[:, :U_CUT], part_u[:, U_CUT:]
    high = jnp.pad(high, ((0, 0), (0, U_CUT - high.shape[1])))
    part = jnp.concatenate([part_w, jnp.concatenate([low, high], axis=0)], axis=1)
    full = lax.all_gather(part, "rep", axis=0, tiled=False)
    return full.reshape(full.shape[0] * full.shape[1], full.shape[2])


def local(
    latents,
    destination,
    token_counts,
    frame_counts,
    gains_spatial,
    gains_temporal,
    qkv_spatial,
    proj_spatial,
    qkv_temporal,
    proj_temporal,
    cotangent,
):
    bins_here, _, slots, width = latents.shape
    groups = lax.axis_size("rep")
    frames = lax.axis_size(SEQ)
    group = lax.axis_index("rep")
    place = lax.axis_index(SEQ)
    inner = proj_spatial.shape[0]
    tokens = bins_here * slots // frames
    rows = bins_here * slots
    sizes = (qkv_spatial.shape[1], proj_spatial.shape[1], width // groups, inner // groups)

    mine = jnp.pad(destination.astype(jnp.bfloat16)[None], ((0, 15), (0, width - bins_here)))
    sent = jnp.concatenate([latents.reshape(rows, width), mine], axis=0)
    shared = lax.all_gather(sent, "rep", axis=0, tiled=False)

    flat_s = own_piece(qkv_spatial, proj_spatial, group, groups)
    flat_s = jnp.pad(flat_s, (0, -flat_s.shape[0] % 256))
    got_s = spread(flat_s.reshape(2, -1), SEQ)

    flat_t = own_piece(qkv_temporal, proj_temporal, group, groups).reshape(tokens, -1)
    flat_t = jnp.pad(flat_t, ((0, 0), (0, -flat_t.shape[1] % 128)))
    mixed = jnp.concatenate(
        [
            cotangent.reshape(frames, tokens, width),
            jnp.broadcast_to(flat_t[None], (frames,) + flat_t.shape),
        ],
        axis=2,
    )
    got_s, mixed = lax.optimization_barrier((got_s, mixed))
    full_s = gather_weights(got_s.reshape(frames, -1), *sizes)
    mixed = exchange(mixed, SEQ)
    piece = sizes[0] * sizes[2] + sizes[1] * sizes[3]
    full_t = gather_weights(
        mixed[:, :, width : width + piece // tokens].reshape(frames, -1), *sizes
    )
    cot_tokens = mixed[:, :, :width].reshape(rows, width)

    dest_all = shared[:, rows, :bins_here].astype(jnp.int32)
    group_ids = jnp.arange(groups, dtype=jnp.int32)
    bin_ids = jnp.arange(bins_here, dtype=jnp.int32)
    here = (dest_all == group).astype(jnp.int32)
    comes = jnp.sum(here, axis=1)
    order = jnp.sum((group_ids[None] < group_ids[:, None]).astype(jnp.int32) * comes[None], axis=1)
    source = (order[None] == bin_ids[:, None]).astype(jnp.int32) * comes[None]
    from_group = jnp.sum(source * group_ids[None], axis=1)
    from_bin = jnp.sum(source * jnp.sum(here * bin_ids[None], axis=1)[None], axis=1)
    earlier = (dest_all[None] == destination[:, None, None]) & (group_ids[None, :, None] < group)
    rank = jnp.sum(earlier.astype(jnp.int32), axis=(1, 2))

    def pick(everyone, groups_of, bins_of):
        return jnp.concatenate(
            [
                lax.dynamic_slice(
                    everyone, (groups_of[i], bins_of[i] * slots, 0), (1, slots, width)
                )[0]
                for i in range(bins_here)
            ]
        )

    moved = pick(shared, from_group, from_bin)
    key_ok = jnp.arange(slots, dtype=jnp.int32)[None, :] < token_counts
    lab_k = jnp.where(key_ok, bin_ids[:, None], -1).reshape(rows, 1)
    lab_q = jnp.broadcast_to(bin_ids[:, None], (bins_here, slots)).reshape(1, rows)
    mid, qkv = call_kernel(spatial_forward_kernel, (ROWS_OUT, QKV_OUT), False, "spatial_forward")(
        moved, gains_spatial, full_s, lab_k, lab_q
    )
    mid_tokens = exchange(mid.reshape(frames, tokens, width), SEQ).reshape(rows, width)

    ends = jnp.cumsum(frame_counts, axis=1)
    video_id = jnp.sum(
        (ends[:, None, :] <= jnp.arange(frames, dtype=jnp.int32)[None, :, None]).astype(jnp.int32),
        axis=2,
    )
    row_bin = place * tokens // slots
    video_row = jnp.sum((bin_ids == row_bin).astype(jnp.int32)[:, None] * video_id, axis=0)
    lab_t = video_row[:, None] * tokens + jnp.arange(tokens, dtype=jnp.int32)[None]
    heads_tokens, mid_grad_tokens, grad_temporal = call_kernel(
        temporal_kernel, (MIXED_OUT, ROWS_OUT, GAIN_OUT), True, "temporal"
    )(cot_tokens, mid_tokens, gains_temporal, full_t, lab_t.reshape(rows, 1), lab_t.reshape(1, rows))

    both = jnp.concatenate([mid_grad_tokens, heads_tokens], axis=1)
    both = exchange(both.reshape(frames, tokens, width + inner), SEQ)
    both = both.reshape(rows, width + inner)
    mid_grad, heads_here = both[:, :width], both[:, width:]
    moved_grad, grad_spatial = call_kernel(
        spatial_backward_kernel, (ROWS_OUT, GAIN_OUT), True, "spatial_backward"
    )(mid_grad, moved, gains_spatial, full_s, lab_k, lab_q, qkv)
    block_out = call_kernel(finish_kernel, ROWS_OUT, False, "finish")(mid, heads_here, full_t)
    returned = lax.all_gather(moved_grad, "rep", axis=0, tiled=False)
    latent_grad = pick(returned, destination, rank)
    sums = jnp.stack([grad_spatial, grad_temporal]).reshape(8, -1)
    for axis in ("y", "z", "rep"):
        sums = jnp.sum(spread(sums, axis), axis=0)
    gain_grads = sums.reshape((2,) + gains_spatial.shape)
    return (block_out.reshape(latents.shape), latent_grad.reshape(latents.shape), gain_grads)


def solution(mesh):
    rep, seq = mesh.devices.shape
    deep = Mesh(mesh.devices.reshape(rep, 8, seq // 8), ("rep", "z", "y"))
    in_specs = (
        P("rep", SEQ, None, None),
        P("rep"),
        P("rep", SEQ),
        P("rep", None),
        P(),
        P(),
        P(None, SEQ),
        P(None, SEQ),
        P(None, SEQ),
        P(None, SEQ),
        P("rep", SEQ, None, None),
    )
    out_specs = (P("rep", SEQ, None, None), P("rep", SEQ, None, None), P())
    return jax.shard_map(local, mesh=deep, in_specs=in_specs, out_specs=out_specs, check_vma=False)
```

```python
import math

import jax
import jax.numpy as jnp
from jax import lax
from jax.experimental import pallas as pl
from jax.experimental.pallas import tpu as pltpu
from jax.sharding import Mesh
from jax.sharding import PartitionSpec as P

HEADS = 8
HD = 72
INNER = HEADS * HD
SEQ = ("z", "y")
CUTS = (0, 640, 1152, 1792, 2304)
U_FROM = 1664


def scores_of(q_ref, k_ref, head, allowed):
    rows = slice(HD * head, HD * head + HD)
    query = q_ref[rows, :].astype(jnp.bfloat16)
    keys = k_ref[rows, :].astype(jnp.bfloat16)
    raw = lax.dot_general(
        keys, query, (((0,), (0,)), ((), ())), preferred_element_type=jnp.float32
    )
    raw = jnp.where(allowed, raw * (1.0 / math.sqrt(HD)), -1000000000.0)
    expo = jnp.exp(raw - jnp.max(raw, axis=0, keepdims=True))
    weights = expo * (1.0 / jnp.sum(expo, axis=0, keepdims=True))
    return query, keys, weights


def normed_of(v_ref):
    wide = v_ref[...].astype(jnp.float32)
    scale = lax.rsqrt(jnp.mean(wide * wide, axis=1, keepdims=True) + 1e-06)
    return wide * scale, scale


def weight_copies(full_hbm, full_ref, sems):
    return [
        pltpu.make_async_copy(
            full_hbm.at[:, CUTS[i] : CUTS[i + 1]], full_ref.at[:, CUTS[i] : CUTS[i + 1]], sems.at[i]
        )
        for i in range(4)
    ]


def load_u(full_ref, u_ref):
    lane = lax.broadcasted_iota(jnp.int32, (72, 128), 1)
    for part in range(8):
        rows = slice(72 * part, 72 * part + 72)
        block = full_ref[144 * part : 144 * part + 144, U_FROM:].astype(jnp.float32)
        left, right = pltpu.roll(block[:72], 576, 1), block[72:]
        u_ref[rows, :512] = left[:, :512]
        u_ref[rows, 512:640] = jnp.where(lane < 64, left[:, 512:], right[:, :128])
        u_ref[rows, 640:] = right[:, 128:]


def forward(v_ref, gains_ref, full_ref, copies, key_label, query_label, q_ref, k_ref, x_ref, o_ref):
    normed, scale = normed_of(v_ref)

    def project(which, first, past):
        copies[which].wait()
        scaled = (normed * gains_ref[which : which + 1, :]).astype(jnp.bfloat16)
        made = jnp.dot(scaled, full_ref[:, first:past], preferred_element_type=jnp.float32)
        return jnp.transpose(made)

    q_ref[...] = project(0, 0, 640)[:INNER]
    k_ref[...] = project(1, 512, 1152)[64:]
    x_ref[...] = project(2, 1152, 1792)[:INNER]
    allowed = key_label == query_label
    for head in range(HEADS):
        rows = slice(HD * head, HD * head + HD)
        _, _, weights = scores_of(q_ref, k_ref, head, allowed)
        vals = x_ref[rows, :].astype(jnp.bfloat16)
        o_ref[rows, :] = jnp.dot(
            vals, weights.astype(jnp.bfloat16), preferred_element_type=jnp.float32
        )
    return jnp.transpose(o_ref[...]).astype(jnp.bfloat16)


def finish(v_ref, mixed, u_ref, out_ref):
    made = jnp.dot(mixed, u_ref[...].astype(jnp.bfloat16), preferred_element_type=jnp.float32)
    out_ref[...] = (v_ref[...].astype(jnp.float32) + made).astype(jnp.bfloat16)


def backward(
    g_ref, v_ref, gains_ref, full_ref, copies, key_label, query_label, grad_ref, gain_ref,
    q_ref, k_ref, x_ref, o_ref, u_ref, dq_ref, dk_ref, dx_ref,
):
    grad = g_ref[...]
    o_ref[...] = lax.dot_general(
        u_ref[...].astype(jnp.bfloat16),
        grad,
        (((1,), (1,)), ((), ())),
        preferred_element_type=jnp.float32,
    )
    zeros = jnp.zeros((640 - INNER, dq_ref.shape[1]), jnp.float32)
    dq_ref[INNER:, :] = zeros
    dk_ref[: 640 - INNER, :] = zeros
    dx_ref[INNER:, :] = zeros
    allowed = key_label == query_label
    over_lanes = (((1,), (1,)), ((), ()))
    for head in range(HEADS):
        low = HD * head
        rows = slice(low, low + HD)
        query, keys, weights = scores_of(q_ref, k_ref, head, allowed)
        vals = x_ref[rows, :].astype(jnp.bfloat16)
        d_out = o_ref[rows, :].astype(jnp.bfloat16)
        d_weights = lax.dot_general(
            vals, d_out, (((0,), (0,)), ((), ())), preferred_element_type=jnp.float32
        )
        along = jnp.sum(d_weights * weights, axis=0, keepdims=True)
        d_scores = weights * (d_weights - along) * (1.0 / math.sqrt(HD))
        d_scores = d_scores.astype(jnp.bfloat16)
        dq_ref[rows, :] = jnp.dot(keys, d_scores, preferred_element_type=jnp.float32)
        dk_ref[64 + low : 64 + low + HD, :] = lax.dot_general(
            query, d_scores, over_lanes, preferred_element_type=jnp.float32
        )
        dx_ref[rows, :] = lax.dot_general(
            d_out, weights.astype(jnp.bfloat16), over_lanes, preferred_element_type=jnp.float32
        )
    normed, scale = normed_of(v_ref)
    for copy in copies:
        copy.wait()
    d_normed = None
    for which, (ref, first) in enumerate(((dq_ref, 0), (dk_ref, 512), (dx_ref, 1152))):
        made = jnp.transpose(ref[...]).astype(jnp.bfloat16)
        back = lax.dot_general(
            made, full_ref[:, first : first + 640], over_lanes, preferred_element_type=jnp.float32
        )
        gain_ref[which : which + 1, :] = jnp.sum(back * normed, axis=0, keepdims=True)
        term = back * gains_ref[which : which + 1, :]
        d_normed = term if d_normed is None else d_normed + term
    inward = jnp.mean(d_normed * normed, axis=1, keepdims=True)
    result = grad.astype(jnp.float32) + scale * (d_normed - normed * inward)
    grad_ref[...] = result.astype(jnp.bfloat16)


def spatial_forward_kernel(
    starts, everyone, gains, full_hbm, lab_k, lab_q, moved, mid, qkv,
    full, sems, u, q, k, x, o, pick_sems,
):
    copies = weight_copies(full_hbm, full, sems)
    picks = [
        pltpu.make_async_copy(
            everyone.at[pl.ds(pl.multiple_of(starts[i], 16), 64), :],
            moved.at[64 * i : 64 * i + 64, :],
            pick_sems.at[i],
        )
        for i in range(4)
    ]
    for copy in picks + copies:
        copy.start()
    for copy in picks:
        copy.wait()
    mixed = forward(moved, gains, full, copies, lab_k[...], lab_q[...], q, k, x, o)
    copies[3].wait()
    load_u(full, u)
    finish(moved, mixed, u, mid)
    for which, ref in enumerate((q, k, x)):
        qkv[which] = ref[...].astype(jnp.bfloat16)


def spatial_backward_kernel(
    g, v, gains, full_hbm, lab_k, lab_q, qkv, grad, gain,
    full, sems, u, q, k, x, o, dq, dk, dx,
):
    copies = weight_copies(full_hbm, full, sems)
    for copy in copies[::-1]:
        copy.start()
    for which, ref in enumerate((q, k, x)):
        ref[...] = qkv[which].astype(jnp.float32)
    copies[3].wait()
    copies[2].wait()
    load_u(full, u)
    backward(
        g, v, gains, full, copies[:2], lab_k[...], lab_q[...], grad, gain,
        q, k, x, o, u, dq, dk, dx,
    )


def temporal_kernel(
    g, v, gains, full_hbm, lab_k, lab_q, mixed, grad, gain,
    full, sems, u, q, k, x, o, dq, dk, dx,
):
    copies = weight_copies(full_hbm, full, sems)
    for copy in copies:
        copy.start()
    mixed[...] = forward(v, gains, full, copies, lab_k[...], lab_q[...], q, k, x, o)
    copies[3].wait()
    load_u(full, u)
    backward(
        g, v, gains, full, [], lab_k[...], lab_q[...], grad, gain, q, k, x, o, u, dq, dk, dx
    )


def finish_kernel(v, mixed, full_hbm, out, full, sems, u):
    copies = weight_copies(full_hbm, full, sems)[2:]
    for copy in copies:
        copy.start()
    for copy in copies:
        copy.wait()
    load_u(full, u)
    finish(v, mixed[...], u, out)


def pick_kernel(starts, everyone, out, sems):
    picks = [
        pltpu.make_async_copy(
            everyone.at[pl.ds(pl.multiple_of(starts[i], 16), 64), :],
            out.at[64 * i : 64 * i + 64, :],
            sems.at[i],
        )
        for i in range(4)
    ]
    for copy in picks:
        copy.start()
    for copy in picks:
        copy.wait()


def call_kernel(kernel, outs, name):
    vmem = pl.BlockSpec(memory_space=pltpu.VMEM)
    smem = pl.BlockSpec(memory_space=pltpu.SMEM)
    hbm = pl.BlockSpec(memory_space=pl.ANY)
    rows = 256
    four = pltpu.SemaphoreType.DMA((4,))
    scratch = [
        pltpu.VMEM((1152, CUTS[-1]), jnp.bfloat16), four, pltpu.VMEM((INNER, 1152), jnp.float32)
    ]
    scratch += [pltpu.VMEM((INNER, rows), jnp.float32)] * 4
    if kernel is finish_kernel:
        ins, scratch = [vmem, vmem, hbm], scratch[:3]
    elif kernel is pick_kernel:
        ins, scratch = [smem, hbm], [four]
    elif kernel is spatial_forward_kernel:
        ins, scratch = [smem, hbm, vmem, hbm, vmem, vmem], scratch + [four]
    else:
        ins = [vmem] * 3 + [hbm] + [vmem] * (2 if kernel is temporal_kernel else 3)
        scratch = scratch + [pltpu.VMEM((640, rows), jnp.float32)] * 3
    return pl.pallas_call(
        kernel,
        out_shape=outs,
        in_specs=ins,
        out_specs=hbm if kernel is pick_kernel else jax.tree.map(lambda _: vmem, outs),
        scratch_shapes=scratch,
        compiler_params=pltpu.CompilerParams(vmem_limit_bytes=50 * 1024 * 1024),
        cost_estimate=pl.CostEstimate(
            flops=int(6e9), bytes_accessed=int(8e6), transcendentals=int(5e5)
        ),
        name=name,
    )


ROWS_OUT = jax.ShapeDtypeStruct((256, 1152), jnp.bfloat16)
MIXED_OUT = jax.ShapeDtypeStruct((256, 576), jnp.bfloat16)
GAIN_OUT = jax.ShapeDtypeStruct((3, 1152), jnp.float32)
QKV_OUT = jax.ShapeDtypeStruct((3, 576, 256), jnp.bfloat16)


def exchange(rows, axes):
    return lax.all_to_all(rows, axes, split_axis=0, concat_axis=0, tiled=True)


def spread(value, axes):
    peers = lax.axis_size(axes)
    return exchange(jnp.broadcast_to(value[None], (peers,) + value.shape), axes)


def own_piece(qkv, proj, rep, groups):
    rows_w, rows_u = qkv.shape[0] // groups, proj.shape[0] // groups
    piece_w = lax.dynamic_slice(qkv.T, (0, rep * rows_w), (qkv.shape[1], rows_w)).reshape(-1)
    piece_u = lax.dynamic_slice(proj.T, (0, rep * rows_u), (proj.shape[1], rows_u)).reshape(-1)
    return jnp.concatenate([piece_w, piece_u])


def gather_weights(got, shard, shard_u, rows_w, rows_u):
    peers = got.shape[0]
    cut = shard * rows_w
    part_w = got[:, :cut].reshape(peers * shard, rows_w).T
    part_u = got[:, cut : cut + shard_u * rows_u].reshape(peers * shard_u, rows_u).T
    half = part_u.shape[1] // 2
    part_u = jnp.concatenate([part_u[:, :half], part_u[:, half:]], axis=0)
    part = jnp.concatenate([part_w, part_u], axis=1)
    full = lax.all_gather(part, "rep", axis=0, tiled=False)
    return full.reshape(full.shape[0] * full.shape[1], full.shape[2])


def local(
    latents,
    destination,
    token_counts,
    frame_counts,
    gains_spatial,
    gains_temporal,
    qkv_spatial,
    proj_spatial,
    qkv_temporal,
    proj_temporal,
    cotangent,
):
    bins_here, _, slots, width = latents.shape
    groups = lax.axis_size("rep")
    frames = lax.axis_size(SEQ)
    group = lax.axis_index("rep")
    place = lax.axis_index(SEQ)
    inner = proj_spatial.shape[0]
    tokens = bins_here * slots // frames
    rows = bins_here * slots
    sizes = (qkv_spatial.shape[1], proj_spatial.shape[1], width // groups, inner // groups)

    mine = jnp.pad(destination.astype(jnp.bfloat16)[None], ((0, 15), (0, width - bins_here)))
    sent = jnp.concatenate([latents.reshape(rows, width), mine], axis=0)
    shared = lax.all_gather(sent, "rep", axis=0, tiled=False)

    flat_s = own_piece(qkv_spatial, proj_spatial, group, groups)
    flat_s = jnp.pad(flat_s, (0, -flat_s.shape[0] % 256))
    got_s = spread(flat_s.reshape(2, -1), SEQ)

    flat_t = own_piece(qkv_temporal, proj_temporal, group, groups).reshape(tokens, -1)
    flat_t = jnp.pad(flat_t, ((0, 0), (0, -flat_t.shape[1] % 128)))
    mixed = jnp.concatenate(
        [
            cotangent.reshape(frames, tokens, width),
            jnp.broadcast_to(flat_t[None], (frames,) + flat_t.shape),
        ],
        axis=2,
    )
    got_s, mixed = lax.optimization_barrier((got_s, mixed))
    full_s = gather_weights(got_s.reshape(frames, -1), *sizes)
    mixed = exchange(mixed, SEQ)
    piece = sizes[0] * sizes[2] + sizes[1] * sizes[3]
    full_t = gather_weights(
        mixed[:, :, width : width + piece // tokens].reshape(frames, -1), *sizes
    )
    cot_tokens = mixed[:, :, :width].reshape(rows, width)

    dest_all = shared[:, rows, :bins_here].astype(jnp.int32)
    group_ids = jnp.arange(groups, dtype=jnp.int32)
    bin_ids = jnp.arange(bins_here, dtype=jnp.int32)
    here = (dest_all == group).astype(jnp.int32)
    comes = jnp.sum(here, axis=1)
    order = jnp.sum((group_ids[None] < group_ids[:, None]).astype(jnp.int32) * comes[None], axis=1)
    source = (order[None] == bin_ids[:, None]).astype(jnp.int32) * comes[None]
    from_group = jnp.sum(source * group_ids[None], axis=1)
    from_bin = jnp.sum(source * jnp.sum(here * bin_ids[None], axis=1)[None], axis=1)
    earlier = (dest_all[None] == destination[:, None, None]) & (group_ids[None, :, None] < group)
    rank = jnp.sum(earlier.astype(jnp.int32), axis=(1, 2))

    starts_here = from_group * shared.shape[1] + from_bin * slots
    starts_back = destination * rows + rank * slots
    key_ok = jnp.arange(slots, dtype=jnp.int32)[None, :] < token_counts
    lab_k = jnp.where(key_ok, bin_ids[:, None], -1).reshape(rows, 1)
    lab_q = jnp.broadcast_to(bin_ids[:, None], (bins_here, slots)).reshape(1, rows)
    moved, mid, qkv = call_kernel(
        spatial_forward_kernel, (ROWS_OUT, ROWS_OUT, QKV_OUT), "spatial_forward"
    )(starts_here, shared.reshape(-1, width), gains_spatial, full_s, lab_k, lab_q)
    mid_tokens = exchange(mid.reshape(frames, tokens, width), SEQ).reshape(rows, width)

    ends = jnp.cumsum(frame_counts, axis=1)
    video_id = jnp.sum(
        (ends[:, None, :] <= jnp.arange(frames, dtype=jnp.int32)[None, :, None]).astype(jnp.int32),
        axis=2,
    )
    row_bin = place * tokens // slots
    video_row = jnp.sum((bin_ids == row_bin).astype(jnp.int32)[:, None] * video_id, axis=0)
    lab_t = video_row[:, None] * tokens + jnp.arange(tokens, dtype=jnp.int32)[None]
    heads_tokens, mid_grad_tokens, grad_temporal = call_kernel(
        temporal_kernel, (MIXED_OUT, ROWS_OUT, GAIN_OUT), "temporal"
    )(cot_tokens, mid_tokens, gains_temporal, full_t, lab_t.reshape(rows, 1), lab_t.reshape(1, rows))

    both = jnp.concatenate([mid_grad_tokens, heads_tokens], axis=1)
    both = exchange(both.reshape(frames, tokens, width + inner), SEQ)
    both = both.reshape(rows, width + inner)
    mid_grad, heads_here = both[:, :width], both[:, width:]
    moved_grad, grad_spatial = call_kernel(
        spatial_backward_kernel, (ROWS_OUT, GAIN_OUT), "spatial_backward"
    )(mid_grad, moved, gains_spatial, full_s, lab_k, lab_q, qkv)
    block_out = call_kernel(finish_kernel, ROWS_OUT, "finish")(mid, heads_here, full_t)
    returned = lax.all_gather(moved_grad, "rep", axis=0, tiled=False)
    latent_grad = call_kernel(pick_kernel, ROWS_OUT, "pick")(
        starts_back, returned.reshape(-1, width)
    )
    sums = jnp.stack([grad_spatial, grad_temporal]).reshape(8, -1)
    for axis in ("y", "z", "rep"):
        sums = jnp.sum(spread(sums, axis), axis=0)
    gain_grads = sums.reshape((2,) + gains_spatial.shape)
    return (block_out.reshape(latents.shape), latent_grad.reshape(latents.shape), gain_grads)


def solution(mesh):
    rep, seq = mesh.devices.shape
    deep = Mesh(mesh.devices.reshape(rep, 8, seq // 8), ("rep", "z", "y"))
    in_specs = (
        P("rep", SEQ, None, None),
        P("rep"),
        P("rep", SEQ),
        P("rep", None),
        P(),
        P(),
        P(None, SEQ),
        P(None, SEQ),
        P(None, SEQ),
        P(None, SEQ),
        P("rep", SEQ, None, None),
    )
    out_specs = (P("rep", SEQ, None, None), P("rep", SEQ, None, None), P())
    return jax.shard_map(local, mesh=deep, in_specs=in_specs, out_specs=out_specs, check_vma=False)
```

```python
import math

import jax
import jax.numpy as jnp
from jax import lax
from jax.experimental import pallas as pl
from jax.experimental.pallas import tpu as pltpu
from jax.sharding import Mesh
from jax.sharding import PartitionSpec as P

HEADS = 8
HD = 72
INNER = HEADS * HD
SEQ = ("z", "y")
CUTS = (0, 640, 1152, 1792, 2304)
U_FROM = 1664


def scores_of(q_ref, k_ref, head, allowed):
    rows = slice(HD * head, HD * head + HD)
    query = q_ref[rows, :].astype(jnp.bfloat16)
    keys = k_ref[rows, :].astype(jnp.bfloat16)
    raw = lax.dot_general(
        keys, query, (((0,), (0,)), ((), ())), preferred_element_type=jnp.float32
    )
    raw = jnp.where(allowed, raw * (1.0 / math.sqrt(HD)), -1000000000.0)
    expo = jnp.exp(raw - jnp.max(raw, axis=0, keepdims=True))
    weights = expo * (1.0 / jnp.sum(expo, axis=0, keepdims=True))
    return query, keys, weights


def normed_of(v_ref):
    wide = v_ref[...].astype(jnp.float32)
    scale = lax.rsqrt(jnp.mean(wide * wide, axis=1, keepdims=True) + 1e-06)
    return wide * scale, scale


def weight_copies(full_hbm, full_ref, sems):
    return [
        pltpu.make_async_copy(
            full_hbm.at[:, CUTS[i] : CUTS[i + 1]], full_ref.at[:, CUTS[i] : CUTS[i + 1]], sems.at[i]
        )
        for i in range(4)
    ]


def load_u(full_ref, u_ref):
    lane = lax.broadcasted_iota(jnp.int32, (72, 128), 1)
    for part in range(8):
        rows = slice(72 * part, 72 * part + 72)
        block = full_ref[144 * part : 144 * part + 144, U_FROM:].astype(jnp.float32)
        left, right = pltpu.roll(block[:72], 576, 1), block[72:]
        u_ref[rows, :512] = left[:, :512]
        u_ref[rows, 512:640] = jnp.where(lane < 64, left[:, 512:], right[:, :128])
        u_ref[rows, 640:] = right[:, 128:]


def forward(v_ref, gains_ref, full_ref, copies, key_label, query_label, q_ref, k_ref, x_ref, o_ref):
    normed, scale = normed_of(v_ref)

    def project(which, first, past):
        copies[which].wait()
        scaled = (normed * gains_ref[which : which + 1, :]).astype(jnp.bfloat16)
        made = jnp.dot(scaled, full_ref[:, first:past], preferred_element_type=jnp.float32)
        return jnp.transpose(made)

    q_ref[...] = project(0, 0, 640)[:INNER]
    k_ref[...] = project(1, 512, 1152)[64:]
    x_ref[...] = project(2, 1152, 1792)[:INNER]
    allowed = key_label == query_label
    for head in range(HEADS):
        rows = slice(HD * head, HD * head + HD)
        _, _, weights = scores_of(q_ref, k_ref, head, allowed)
        vals = x_ref[rows, :].astype(jnp.bfloat16)
        o_ref[rows, :] = jnp.dot(
            vals, weights.astype(jnp.bfloat16), preferred_element_type=jnp.float32
        )
    return jnp.transpose(o_ref[...]).astype(jnp.bfloat16)


def finish(v_ref, mixed, u_ref, out_ref):
    made = jnp.dot(mixed, u_ref[...].astype(jnp.bfloat16), preferred_element_type=jnp.float32)
    made = (v_ref[...].astype(jnp.float32) + made).astype(jnp.bfloat16)
    out_ref[...] = made.reshape(out_ref.shape)


def backward(
    g_ref, v_ref, gains_ref, full_ref, copies, key_label, query_label, grad_ref, gain_ref,
    q_ref, k_ref, x_ref, o_ref, u_ref, dq_ref, dk_ref, dx_ref,
):
    grad = g_ref[...]
    o_ref[...] = lax.dot_general(
        u_ref[...].astype(jnp.bfloat16),
        grad,
        (((1,), (1,)), ((), ())),
        preferred_element_type=jnp.float32,
    )
    zeros = jnp.zeros((640 - INNER, dq_ref.shape[1]), jnp.float32)
    dq_ref[INNER:, :] = zeros
    dk_ref[: 640 - INNER, :] = zeros
    dx_ref[INNER:, :] = zeros
    allowed = key_label == query_label
    over_lanes = (((1,), (1,)), ((), ()))
    for head in range(HEADS):
        low = HD * head
        rows = slice(low, low + HD)
        query, keys, weights = scores_of(q_ref, k_ref, head, allowed)
        vals = x_ref[rows, :].astype(jnp.bfloat16)
        d_out = o_ref[rows, :].astype(jnp.bfloat16)
        d_weights = lax.dot_general(
            vals, d_out, (((0,), (0,)), ((), ())), preferred_element_type=jnp.float32
        )
        along = jnp.sum(d_weights * weights, axis=0, keepdims=True)
        d_scores = weights * (d_weights - along) * (1.0 / math.sqrt(HD))
        d_scores = d_scores.astype(jnp.bfloat16)
        dq_ref[rows, :] = jnp.dot(keys, d_scores, preferred_element_type=jnp.float32)
        dk_ref[64 + low : 64 + low + HD, :] = lax.dot_general(
            query, d_scores, over_lanes, preferred_element_type=jnp.float32
        )
        dx_ref[rows, :] = lax.dot_general(
            d_out, weights.astype(jnp.bfloat16), over_lanes, preferred_element_type=jnp.float32
        )
    normed, scale = normed_of(v_ref)
    for copy in copies:
        copy.wait()
    d_normed = None
    for which, (ref, first) in enumerate(((dq_ref, 0), (dk_ref, 512), (dx_ref, 1152))):
        made = jnp.transpose(ref[...]).astype(jnp.bfloat16)
        back = lax.dot_general(
            made, full_ref[:, first : first + 640], over_lanes, preferred_element_type=jnp.float32
        )
        gain_ref[which : which + 1, :] = jnp.sum(back * normed, axis=0, keepdims=True)
        term = back * gains_ref[which : which + 1, :]
        d_normed = term if d_normed is None else d_normed + term
    inward = jnp.mean(d_normed * normed, axis=1, keepdims=True)
    result = grad.astype(jnp.float32) + scale * (d_normed - normed * inward)
    grad_ref[...] = result.astype(jnp.bfloat16)


def spatial_forward_kernel(
    starts, everyone, gains, full_hbm, lab_k, lab_q, moved, mid, qkv,
    full, sems, u, q, k, x, o, pick_sems,
):
    copies = weight_copies(full_hbm, full, sems)
    picks = [
        pltpu.make_async_copy(
            everyone.at[pl.ds(pl.multiple_of(starts[i], 16), 64), :],
            moved.at[64 * i : 64 * i + 64, :],
            pick_sems.at[i],
        )
        for i in range(4)
    ]
    for copy in picks + copies:
        copy.start()
    for copy in picks:
        copy.wait()
    mixed = forward(moved, gains, full, copies, lab_k[...], lab_q[...], q, k, x, o)
    copies[3].wait()
    load_u(full, u)
    finish(moved, mixed, u, mid)
    for which, ref in enumerate((q, k, x)):
        qkv[which] = ref[...].astype(jnp.bfloat16)


def spatial_backward_kernel(
    both, v, gains, full_hbm, lab_k, lab_q, qkv, grad, gain,
    full, sems, u, q, k, x, o, dq, dk, dx, g,
):
    copies = weight_copies(full_hbm, full, sems)
    for copy in copies[::-1]:
        copy.start()
    for which, ref in enumerate((q, k, x)):
        ref[...] = qkv[which].astype(jnp.float32)
    g[...] = both[:, :, :1152].reshape(g.shape)
    copies[3].wait()
    copies[2].wait()
    load_u(full, u)
    backward(
        g, v, gains, full, copies[:2], lab_k[...], lab_q[...], grad, gain,
        q, k, x, o, u, dq, dk, dx,
    )


def temporal_kernel(
    got, mid, gains, full_hbm, lab_k, lab_q, both, gain,
    full, sems, u, q, k, x, o, dq, dk, dx, g, v, grad,
):
    copies = weight_copies(full_hbm, full, sems)
    for copy in copies:
        copy.start()
    v[...] = mid[...].reshape(v.shape)
    g[...] = got[:, :, :1152].reshape(g.shape)
    mixed = forward(v, gains, full, copies, lab_k[...], lab_q[...], q, k, x, o)
    both[:, :, 1152:] = mixed.reshape(both.shape[0], both.shape[1], INNER)
    copies[3].wait()
    load_u(full, u)
    backward(
        g, v, gains, full, [], lab_k[...], lab_q[...], grad, gain, q, k, x, o, u, dq, dk, dx
    )
    both[:, :, :1152] = grad[...].reshape(both.shape[0], both.shape[1], 1152)


def finish_kernel(mid, both, full_hbm, out, full, sems, u, v):
    copies = weight_copies(full_hbm, full, sems)[2:]
    for copy in copies:
        copy.start()
    v[...] = mid[...].reshape(v.shape)
    mixed = both[:, :, 1152:].reshape(v.shape[0], INNER)
    for copy in copies:
        copy.wait()
    load_u(full, u)
    finish(v, mixed, u, out)


def pick_kernel(starts, everyone, out, sems):
    picks = [
        pltpu.make_async_copy(
            everyone.at[pl.ds(pl.multiple_of(starts[i], 16), 64), :],
            out.at[64 * i : 64 * i + 64, :],
            sems.at[i],
        )
        for i in range(4)
    ]
    for copy in picks:
        copy.start()
    for copy in picks:
        copy.wait()


def call_kernel(kernel, outs, name):
    vmem = pl.BlockSpec(memory_space=pltpu.VMEM)
    smem = pl.BlockSpec(memory_space=pltpu.SMEM)
    hbm = pl.BlockSpec(memory_space=pl.ANY)
    rows = 256
    four = pltpu.SemaphoreType.DMA((4,))
    scratch = [
        pltpu.VMEM((1152, CUTS[-1]), jnp.bfloat16), four, pltpu.VMEM((INNER, 1152), jnp.float32)
    ]
    scratch += [pltpu.VMEM((INNER, rows), jnp.float32)] * 4
    flat = pltpu.VMEM((rows, 1152), jnp.bfloat16)
    backs = [pltpu.VMEM((640, rows), jnp.float32)] * 3
    if kernel is finish_kernel:
        ins, scratch = [vmem, vmem, hbm], scratch[:3] + [flat]
    elif kernel is pick_kernel:
        ins, scratch = [smem, hbm], [four]
    elif kernel is spatial_forward_kernel:
        ins, scratch = [smem, hbm, vmem, hbm, vmem, vmem], scratch + [four]
    elif kernel is temporal_kernel:
        ins, scratch = [vmem] * 3 + [hbm] + [vmem] * 2, scratch + backs + [flat] * 3
    else:
        ins, scratch = [vmem] * 3 + [hbm] + [vmem] * 3, scratch + backs + [flat]
    return pl.pallas_call(
        kernel,
        out_shape=outs,
        in_specs=ins,
        out_specs=jax.tree.map(lambda _: vmem, outs),
        scratch_shapes=scratch,
        compiler_params=pltpu.CompilerParams(vmem_limit_bytes=50 * 1024 * 1024),
        cost_estimate=pl.CostEstimate(
            flops=int(6e9), bytes_accessed=int(8e6), transcendentals=int(5e5)
        ),
        name=name,
    )


ROWS_OUT = jax.ShapeDtypeStruct((256, 1152), jnp.bfloat16)
MID_OUT = jax.ShapeDtypeStruct((64, 4, 1152), jnp.bfloat16)
BOTH_OUT = jax.ShapeDtypeStruct((64, 4, 1728), jnp.bfloat16)
GAIN_OUT = jax.ShapeDtypeStruct((3, 1152), jnp.float32)
QKV_OUT = jax.ShapeDtypeStruct((3, 576, 256), jnp.bfloat16)


def exchange(rows, axes):
    return lax.all_to_all(rows, axes, split_axis=0, concat_axis=0, tiled=True)


def spread(value, axes):
    peers = lax.axis_size(axes)
    return exchange(jnp.broadcast_to(value[None], (peers,) + value.shape), axes)


def own_piece(qkv, proj, rep, groups):
    rows_w, rows_u = qkv.shape[0] // groups, proj.shape[0] // groups
    piece_w = lax.dynamic_slice(qkv.T, (0, rep * rows_w), (qkv.shape[1], rows_w)).reshape(-1)
    piece_u = lax.dynamic_slice(proj.T, (0, rep * rows_u), (proj.shape[1], rows_u)).reshape(-1)
    return jnp.concatenate([piece_w, piece_u])


def gather_weights(got, shard, shard_u, rows_w, rows_u):
    peers = got.shape[0]
    cut = shard * rows_w
    part_w = got[:, :cut].reshape(peers * shard, rows_w).T
    part_u = got[:, cut : cut + shard_u * rows_u].reshape(peers * shard_u, rows_u).T
    half = part_u.shape[1] // 2
    part_u = jnp.concatenate([part_u[:, :half], part_u[:, half:]], axis=0)
    part = jnp.concatenate([part_w, part_u], axis=1)
    full = lax.all_gather(part, "rep", axis=0, tiled=False)
    return full.reshape(full.shape[0] * full.shape[1], full.shape[2])


def local(
    latents,
    destination,
    token_counts,
    frame_counts,
    gains_spatial,
    gains_temporal,
    qkv_spatial,
    proj_spatial,
    qkv_temporal,
    proj_temporal,
    cotangent,
):
    bins_here, _, slots, width = latents.shape
    groups = lax.axis_size("rep")
    frames = lax.axis_size(SEQ)
    group = lax.axis_index("rep")
    place = lax.axis_index(SEQ)
    inner = proj_spatial.shape[0]
    tokens = bins_here * slots // frames
    rows = bins_here * slots
    sizes = (qkv_spatial.shape[1], proj_spatial.shape[1], width // groups, inner // groups)

    mine = jnp.pad(destination.astype(jnp.bfloat16)[None], ((0, 15), (0, width - bins_here)))
    sent = jnp.concatenate([latents.reshape(rows, width), mine], axis=0)
    shared = lax.all_gather(sent, "rep", axis=0, tiled=False)

    flat_s = own_piece(qkv_spatial, proj_spatial, group, groups)
    flat_s = jnp.pad(flat_s, (0, -flat_s.shape[0] % 256))
    got_s = spread(flat_s.reshape(2, -1), SEQ)

    flat_t = own_piece(qkv_temporal, proj_temporal, group, groups).reshape(tokens, -1)
    flat_t = jnp.pad(flat_t, ((0, 0), (0, -flat_t.shape[1] % 128)))
    mixed = jnp.concatenate(
        [
            cotangent.reshape(frames, tokens, width),
            jnp.broadcast_to(flat_t[None], (frames,) + flat_t.shape),
        ],
        axis=2,
    )
    got_s, mixed = lax.optimization_barrier((got_s, mixed))
    full_s = gather_weights(got_s.reshape(frames, -1), *sizes)
    mixed = exchange(mixed, SEQ)
    piece = sizes[0] * sizes[2] + sizes[1] * sizes[3]
    full_t = gather_weights(
        mixed[:, :, width : width + piece // tokens].reshape(frames, -1), *sizes
    )

    dest_all = shared[:, rows, :bins_here].astype(jnp.int32)
    group_ids = jnp.arange(groups, dtype=jnp.int32)
    bin_ids = jnp.arange(bins_here, dtype=jnp.int32)
    here = (dest_all == group).astype(jnp.int32)
    comes = jnp.sum(here, axis=1)
    order = jnp.sum((group_ids[None] < group_ids[:, None]).astype(jnp.int32) * comes[None], axis=1)
    source = (order[None] == bin_ids[:, None]).astype(jnp.int32) * comes[None]
    from_group = jnp.sum(source * group_ids[None], axis=1)
    from_bin = jnp.sum(source * jnp.sum(here * bin_ids[None], axis=1)[None], axis=1)
    earlier = (dest_all[None] == destination[:, None, None]) & (group_ids[None, :, None] < group)
    rank = jnp.sum(earlier.astype(jnp.int32), axis=(1, 2))

    starts_here = from_group * shared.shape[1] + from_bin * slots
    starts_back = destination * rows + rank * slots
    key_ok = jnp.arange(slots, dtype=jnp.int32)[None, :] < token_counts
    lab_k = jnp.where(key_ok, bin_ids[:, None], -1).reshape(rows, 1)
    lab_q = jnp.broadcast_to(bin_ids[:, None], (bins_here, slots)).reshape(1, rows)
    moved, mid, qkv = call_kernel(
        spatial_forward_kernel, (ROWS_OUT, MID_OUT, QKV_OUT), "spatial_forward"
    )(starts_here, shared.reshape(-1, width), gains_spatial, full_s, lab_k, lab_q)
    mid_tokens = exchange(mid, SEQ)

    ends = jnp.cumsum(frame_counts, axis=1)
    video_id = jnp.sum(
        (ends[:, None, :] <= jnp.arange(frames, dtype=jnp.int32)[None, :, None]).astype(jnp.int32),
        axis=2,
    )
    row_bin = place * tokens // slots
    video_row = jnp.sum((bin_ids == row_bin).astype(jnp.int32)[:, None] * video_id, axis=0)
    lab_t = video_row[:, None] * tokens + jnp.arange(tokens, dtype=jnp.int32)[None]
    both, grad_temporal = call_kernel(temporal_kernel, (BOTH_OUT, GAIN_OUT), "temporal")(
        mixed, mid_tokens, gains_temporal, full_t, lab_t.reshape(rows, 1), lab_t.reshape(1, rows)
    )
    both = exchange(both, SEQ)
    moved_grad, grad_spatial = call_kernel(
        spatial_backward_kernel, (ROWS_OUT, GAIN_OUT), "spatial_backward"
    )(both, moved, gains_spatial, full_s, lab_k, lab_q, qkv)
    block_out = call_kernel(finish_kernel, ROWS_OUT, "finish")(mid, both, full_t)
    returned = lax.all_gather(moved_grad, "rep", axis=0, tiled=False)
    latent_grad = call_kernel(pick_kernel, ROWS_OUT, "pick")(
        starts_back, returned.reshape(-1, width)
    )
    sums = jnp.stack([grad_spatial, grad_temporal]).reshape(-1, 128)
    for axis in ("y", "z", "rep"):
        sums = jnp.sum(spread(sums, axis), axis=0)
    gain_grads = sums.reshape((2,) + gains_spatial.shape)
    return (block_out.reshape(latents.shape), latent_grad.reshape(latents.shape), gain_grads)


def solution(mesh):
    rep, seq = mesh.devices.shape
    deep = Mesh(mesh.devices.reshape(rep, 8, seq // 8), ("rep", "z", "y"))
    in_specs = (
        P("rep", SEQ, None, None),
        P("rep"),
        P("rep", SEQ),
        P("rep", None),
        P(),
        P(),
        P(None, SEQ),
        P(None, SEQ),
        P(None, SEQ),
        P(None, SEQ),
        P("rep", SEQ, None, None),
    )
    out_specs = (P("rep", SEQ, None, None), P("rep", SEQ, None, None), P())
    return jax.shard_map(local, mesh=deep, in_specs=in_specs, out_specs=out_specs, check_vma=False)
```

```python
import math

import jax
import jax.numpy as jnp
from jax import lax
from jax.experimental import pallas as pl
from jax.experimental.pallas import tpu as pltpu
from jax.sharding import Mesh
from jax.sharding import PartitionSpec as P

HEADS = 8
HD = 72
INNER = HEADS * HD
SEQ = ("z", "y")
CUTS = (0, 640, 1152, 1792, 2304)
U_FROM = 1664


OVER_ROWS = (((0,), (0,)), ((), ()))
OVER_LANES = (((1,), (1,)), ((), ()))
TO_POWER = math.log2(math.e) / math.sqrt(HD)


def softmax_of(raw, allowed):
    raw = jnp.where(allowed, raw * TO_POWER, -1000000000.0)
    expo = jnp.exp2(raw - jnp.max(raw, axis=0, keepdims=True))
    return expo * (1.0 / jnp.sum(expo, axis=0, keepdims=True))


def frame_blocks(left, right):
    lane = lax.broadcasted_iota(jnp.int32, (64, 128), 1)
    halves = []
    for half in range(2):
        lanes = slice(128 * half, 128 * half + 128)
        made = lax.dot_general(
            left[:, lanes], right[:, lanes], OVER_ROWS, preferred_element_type=jnp.float32
        )
        halves.append(jnp.where(lane < 64, made[:64], made[64:]))
    return jnp.concatenate(halves, axis=1)


def spread_blocks(blocks):
    lane = lax.broadcasted_iota(jnp.int32, (64, 128), 1)
    squares = []
    for half in range(2):
        block = blocks[:, 128 * half : 128 * half + 128]
        pair = [jnp.where(lane < 64, block, 0.0), jnp.where(lane < 64, 0.0, block)]
        squares.append(jnp.concatenate(pair, axis=0).astype(jnp.bfloat16))
    return squares


def times_squares(left, squares, dims):
    made = [
        lax.dot_general(
            left[:, 128 * half : 128 * half + 128], squares[half], dims,
            preferred_element_type=jnp.float32,
        )
        for half in range(2)
    ]
    return jnp.concatenate(made, axis=1)


FORWARD_DIMS = (((1,), (0,)), ((), ()))


def normed_of(v_ref):
    wide = v_ref[...].astype(jnp.float32)
    scale = lax.rsqrt(jnp.mean(wide * wide, axis=1, keepdims=True) + 1e-06)
    return wide * scale, scale


def weight_copies(full_hbm, full_ref, sems):
    return [
        pltpu.make_async_copy(
            full_hbm.at[:, CUTS[i] : CUTS[i + 1]], full_ref.at[:, CUTS[i] : CUTS[i + 1]], sems.at[i]
        )
        for i in range(4)
    ]


def load_u(full_ref, u_ref):
    lane = lax.broadcasted_iota(jnp.int32, (72, 128), 1)
    for part in range(8):
        rows = slice(72 * part, 72 * part + 72)
        block = full_ref[144 * part : 144 * part + 144, U_FROM:].astype(jnp.float32)
        left, right = pltpu.roll(block[:72], 576, 1), block[72:]
        u_ref[rows, :512] = left[:, :512]
        u_ref[rows, 512:640] = jnp.where(lane < 64, left[:, 512:], right[:, :128])
        u_ref[rows, 640:] = right[:, 128:]


def forward(v_ref, gains_ref, full_ref, copies, allowed, q_ref, k_ref, x_ref, o_ref, w_ref):
    normed, scale = normed_of(v_ref)

    def project(which, first, past):
        copies[which].wait()
        scaled = (normed * gains_ref[which : which + 1, :]).astype(jnp.bfloat16)
        made = jnp.dot(scaled, full_ref[:, first:past], preferred_element_type=jnp.float32)
        return jnp.transpose(made.astype(jnp.bfloat16)).astype(jnp.float32)

    q_ref[...] = project(0, 0, 640)[:INNER]
    k_ref[...] = project(1, 512, 1152)[64:]
    x_ref[...] = project(2, 1152, 1792)[:INNER]
    for head in range(HEADS):
        rows = slice(HD * head, HD * head + HD)
        query = q_ref[rows, :].astype(jnp.bfloat16)
        keys = k_ref[rows, :].astype(jnp.bfloat16)
        vals = x_ref[rows, :].astype(jnp.bfloat16)
        if w_ref is None:
            weights = softmax_of(frame_blocks(keys, query), allowed)
            o_ref[rows, :] = times_squares(vals, spread_blocks(weights), FORWARD_DIMS)
        else:
            raw = lax.dot_general(keys, query, OVER_ROWS, preferred_element_type=jnp.float32)
            weights = softmax_of(raw, allowed)
            w_ref[head] = weights
            o_ref[rows, :] = jnp.dot(
                vals, weights.astype(jnp.bfloat16), preferred_element_type=jnp.float32
            )
    return jnp.transpose(o_ref[...]).astype(jnp.bfloat16)


def finish(v_ref, mixed, u_ref, out_ref):
    made = jnp.dot(mixed, u_ref[...].astype(jnp.bfloat16), preferred_element_type=jnp.float32)
    made = (v_ref[...].astype(jnp.float32) + made).astype(jnp.bfloat16)
    out_ref[...] = made.reshape(out_ref.shape)


def backward(
    g_ref, v_ref, gains_ref, full_ref, copies, allowed, grad_ref, gain_ref,
    q_ref, k_ref, x_ref, o_ref, u_ref, dq_ref, dk_ref, dx_ref, w_ref,
):
    grad = g_ref[...]
    o_ref[...] = lax.dot_general(
        u_ref[...].astype(jnp.bfloat16),
        grad,
        (((1,), (1,)), ((), ())),
        preferred_element_type=jnp.float32,
    )
    zeros = jnp.zeros((640 - INNER, dq_ref.shape[1]), jnp.float32)
    dq_ref[INNER:, :] = zeros
    dk_ref[: 640 - INNER, :] = zeros
    dx_ref[INNER:, :] = zeros
    for head in range(HEADS):
        low = HD * head
        rows = slice(low, low + HD)
        query = q_ref[rows, :].astype(jnp.bfloat16)
        keys = k_ref[rows, :].astype(jnp.bfloat16)
        vals = x_ref[rows, :].astype(jnp.bfloat16)
        d_out = o_ref[rows, :].astype(jnp.bfloat16)
        if w_ref is None:
            weights = softmax_of(frame_blocks(keys, query), allowed)
            d_weights = frame_blocks(vals, d_out)
        else:
            weights = w_ref[head]
            d_weights = lax.dot_general(
                vals, d_out, OVER_ROWS, preferred_element_type=jnp.float32
            )
        along = jnp.sum(d_weights * weights, axis=0, keepdims=True)
        d_scores = weights * ((d_weights - along) * (1.0 / math.sqrt(HD)))
        if w_ref is None:
            d_scores, weights = spread_blocks(d_scores), spread_blocks(weights)
            dq = times_squares(keys, d_scores, FORWARD_DIMS)
            dk = times_squares(query, d_scores, OVER_LANES)
            dx = times_squares(d_out, weights, OVER_LANES)
        else:
            d_scores, weights = d_scores.astype(jnp.bfloat16), weights.astype(jnp.bfloat16)
            dq = jnp.dot(keys, d_scores, preferred_element_type=jnp.float32)
            dk = lax.dot_general(query, d_scores, OVER_LANES, preferred_element_type=jnp.float32)
            dx = lax.dot_general(d_out, weights, OVER_LANES, preferred_element_type=jnp.float32)
        dq_ref[rows, :] = dq
        dk_ref[64 + low : 64 + low + HD, :] = dk
        dx_ref[rows, :] = dx
    normed, scale = normed_of(v_ref)
    for copy in copies:
        copy.wait()
    d_normed = None
    for which, (ref, first) in enumerate(((dq_ref, 0), (dk_ref, 512), (dx_ref, 1152))):
        made = jnp.transpose(ref[...]).astype(jnp.bfloat16)
        back = lax.dot_general(
            made, full_ref[:, first : first + 640], OVER_LANES, preferred_element_type=jnp.float32
        )
        gain_ref[which : which + 1, :] = jnp.sum(back * normed, axis=0, keepdims=True)
        term = back * gains_ref[which : which + 1, :]
        d_normed = term if d_normed is None else d_normed + term
    inward = jnp.mean(d_normed * normed, axis=1, keepdims=True)
    result = grad.astype(jnp.float32) + scale * (d_normed - normed * inward)
    grad_ref[...] = result.astype(jnp.bfloat16)


def valid_keys(counts):
    return lax.broadcasted_iota(jnp.int32, (64, 256), 0) < counts[...]


def spatial_forward_kernel(
    starts, everyone, gains, full_hbm, counts, moved, mid, qkv,
    full, sems, u, q, k, x, o, pick_sems,
):
    copies = weight_copies(full_hbm, full, sems)
    picks = [
        pltpu.make_async_copy(
            everyone.at[pl.ds(pl.multiple_of(starts[i], 16), 64), :],
            moved.at[64 * i : 64 * i + 64, :],
            pick_sems.at[i],
        )
        for i in range(4)
    ]
    for copy in picks + copies[:1]:
        copy.start()
    for copy in picks:
        copy.wait()
    for copy in copies[1:]:
        copy.start()
    mixed = forward(moved, gains, full, copies, valid_keys(counts), q, k, x, o, None)
    copies[3].wait()
    load_u(full, u)
    finish(moved, mixed, u, mid)
    for which, ref in enumerate((q, k, x)):
        qkv[which] = ref[...].astype(jnp.bfloat16)


def spatial_backward_kernel(
    both, v, gains, full_hbm, counts, qkv, grad, gain,
    full, sems, u, q, k, x, o, dq, dk, dx, g,
):
    copies = weight_copies(full_hbm, full, sems)
    for copy in copies[::-1]:
        copy.start()
    for which, ref in enumerate((q, k, x)):
        ref[...] = qkv[which].astype(jnp.float32)
    g[...] = both[:, :, :1152].reshape(g.shape)
    copies[3].wait()
    copies[2].wait()
    load_u(full, u)
    backward(
        g, v, gains, full, copies[:2], valid_keys(counts), grad, gain,
        q, k, x, o, u, dq, dk, dx, None,
    )


def temporal_kernel(
    got, mid, gains, full_hbm, lab_k, lab_q, both, gain,
    full, sems, u, q, k, x, o, dq, dk, dx, g, v, grad, w,
):
    copies = weight_copies(full_hbm, full, sems)
    for copy in copies:
        copy.start()
    v[...] = mid[...].reshape(v.shape)
    g[...] = got[:, :, :1152].reshape(g.shape)
    allowed = lab_k[...] == lab_q[...]
    mixed = forward(v, gains, full, copies, allowed, q, k, x, o, w)
    both[:, :, 1152:] = mixed.reshape(both.shape[0], both.shape[1], INNER)
    copies[3].wait()
    load_u(full, u)
    backward(
        g, v, gains, full, [], allowed, grad, gain, q, k, x, o, u, dq, dk, dx, w
    )
    both[:, :, :1152] = grad[...].reshape(both.shape[0], both.shape[1], 1152)


def finish_kernel(mid, both, full_hbm, out, full, sems, u, v):
    copies = weight_copies(full_hbm, full, sems)[2:]
    for copy in copies:
        copy.start()
    v[...] = mid[...].reshape(v.shape)
    mixed = both[:, :, 1152:].reshape(v.shape[0], INNER)
    for copy in copies:
        copy.wait()
    load_u(full, u)
    finish(v, mixed, u, out)


def pick_kernel(starts, everyone, out, sems):
    picks = [
        pltpu.make_async_copy(
            everyone.at[pl.ds(pl.multiple_of(starts[i], 16), 64), :],
            out.at[64 * i : 64 * i + 64, :],
            sems.at[i],
        )
        for i in range(4)
    ]
    for copy in picks:
        copy.start()
    for copy in picks:
        copy.wait()


def call_kernel(kernel, outs, name):
    vmem = pl.BlockSpec(memory_space=pltpu.VMEM)
    smem = pl.BlockSpec(memory_space=pltpu.SMEM)
    hbm = pl.BlockSpec(memory_space=pl.ANY)
    rows = 256
    four = pltpu.SemaphoreType.DMA((4,))
    scratch = [
        pltpu.VMEM((1152, CUTS[-1]), jnp.bfloat16), four, pltpu.VMEM((INNER, 1152), jnp.float32)
    ]
    scratch += [pltpu.VMEM((INNER, rows), jnp.float32)] * 4
    flat = pltpu.VMEM((rows, 1152), jnp.bfloat16)
    backs = [pltpu.VMEM((640, rows), jnp.float32)] * 3
    if kernel is finish_kernel:
        ins, scratch = [vmem, vmem, hbm], scratch[:3] + [flat]
    elif kernel is pick_kernel:
        ins, scratch = [smem, hbm], [four]
    elif kernel is spatial_forward_kernel:
        ins, scratch = [smem, hbm, vmem, hbm, vmem], scratch + [four]
    elif kernel is temporal_kernel:
        ins, scratch = [vmem] * 3 + [hbm] + [vmem] * 2, scratch + backs + [flat] * 3
        scratch = scratch + [pltpu.VMEM((HEADS, rows, rows), jnp.float32)]
    else:
        ins, scratch = [vmem] * 3 + [hbm] + [vmem] * 2, scratch + backs + [flat]
    return pl.pallas_call(
        kernel,
        out_shape=outs,
        in_specs=ins,
        out_specs=jax.tree.map(lambda _: vmem, outs),
        scratch_shapes=scratch,
        compiler_params=pltpu.CompilerParams(vmem_limit_bytes=50 * 1024 * 1024),
        cost_estimate=pl.CostEstimate(
            flops=int(6e9), bytes_accessed=int(8e6), transcendentals=int(5e5)
        ),
        name=name,
    )


ROWS_OUT = jax.ShapeDtypeStruct((256, 1152), jnp.bfloat16)
MID_OUT = jax.ShapeDtypeStruct((64, 4, 1152), jnp.bfloat16)
BOTH_OUT = jax.ShapeDtypeStruct((64, 4, 1728), jnp.bfloat16)
GAIN_OUT = jax.ShapeDtypeStruct((3, 1152), jnp.float32)
QKV_OUT = jax.ShapeDtypeStruct((3, 576, 256), jnp.bfloat16)


def exchange(rows, axes):
    return lax.all_to_all(rows, axes, split_axis=0, concat_axis=0, tiled=True)


def spread(value, axes):
    peers = lax.axis_size(axes)
    return exchange(jnp.broadcast_to(value[None], (peers,) + value.shape), axes)


def own_piece(qkv, proj, rep, groups):
    rows_w, rows_u = qkv.shape[0] // groups, proj.shape[0] // groups
    piece_w = lax.dynamic_slice(qkv.T, (0, rep * rows_w), (qkv.shape[1], rows_w)).reshape(-1)
    piece_u = lax.dynamic_slice(proj.T, (0, rep * rows_u), (proj.shape[1], rows_u)).reshape(-1)
    return jnp.concatenate([piece_w, piece_u])


def gather_weights(got, shard, shard_u, rows_w, rows_u):
    peers = got.shape[0]
    cut = shard * rows_w
    part_w = got[:, :cut].reshape(peers * shard, rows_w).T
    part_u = got[:, cut : cut + shard_u * rows_u].reshape(peers * shard_u, rows_u).T
    half = part_u.shape[1] // 2
    part_u = jnp.concatenate([part_u[:, :half], part_u[:, half:]], axis=0)
    part = jnp.concatenate([part_w, part_u], axis=1)
    full = lax.all_gather(part, "rep", axis=0, tiled=False)
    return full.reshape(full.shape[0] * full.shape[1], full.shape[2])


def local(
    latents,
    destination,
    token_counts,
    frame_counts,
    gains_spatial,
    gains_temporal,
    qkv_spatial,
    proj_spatial,
    qkv_temporal,
    proj_temporal,
    cotangent,
):
    bins_here, _, slots, width = latents.shape
    groups = lax.axis_size("rep")
    frames = lax.axis_size(SEQ)
    group = lax.axis_index("rep")
    place = lax.axis_index(SEQ)
    inner = proj_spatial.shape[0]
    tokens = bins_here * slots // frames
    rows = bins_here * slots
    sizes = (qkv_spatial.shape[1], proj_spatial.shape[1], width // groups, inner // groups)

    mine = jnp.pad(destination.astype(jnp.bfloat16)[None], ((0, 15), (0, width - bins_here)))
    sent = jnp.concatenate([latents.reshape(rows, width), mine], axis=0)
    shared = lax.all_gather(sent, "rep", axis=0, tiled=False)

    flat_s = own_piece(qkv_spatial, proj_spatial, group, groups)
    flat_s = jnp.pad(flat_s, (0, -flat_s.shape[0] % 256))
    got_s = spread(flat_s.reshape(2, -1), SEQ)

    flat_t = own_piece(qkv_temporal, proj_temporal, group, groups).reshape(tokens, -1)
    flat_t = jnp.pad(flat_t, ((0, 0), (0, -flat_t.shape[1] % 128)))
    mixed = jnp.concatenate(
        [
            cotangent.reshape(frames, tokens, width),
            jnp.broadcast_to(flat_t[None], (frames,) + flat_t.shape),
        ],
        axis=2,
    )
    got_s, mixed = lax.optimization_barrier((got_s, mixed))
    full_s = gather_weights(got_s.reshape(frames, -1), *sizes)
    mixed = exchange(mixed, SEQ)
    piece = sizes[0] * sizes[2] + sizes[1] * sizes[3]
    full_t = gather_weights(
        mixed[:, :, width : width + piece // tokens].reshape(frames, -1), *sizes
    )

    dest_all = shared[:, rows, :bins_here].astype(jnp.int32)
    group_ids = jnp.arange(groups, dtype=jnp.int32)
    bin_ids = jnp.arange(bins_here, dtype=jnp.int32)
    here = (dest_all == group).astype(jnp.int32)
    comes = jnp.sum(here, axis=1)
    order = jnp.sum((group_ids[None] < group_ids[:, None]).astype(jnp.int32) * comes[None], axis=1)
    source = (order[None] == bin_ids[:, None]).astype(jnp.int32) * comes[None]
    from_group = jnp.sum(source * group_ids[None], axis=1)
    from_bin = jnp.sum(source * jnp.sum(here * bin_ids[None], axis=1)[None], axis=1)
    earlier = (dest_all[None] == destination[:, None, None]) & (group_ids[None, :, None] < group)
    rank = jnp.sum(earlier.astype(jnp.int32), axis=(1, 2))

    starts_here = from_group * shared.shape[1] + from_bin * slots
    starts_back = destination * rows + rank * slots
    counts = jnp.broadcast_to(token_counts, (bins_here, slots)).reshape(1, rows)
    moved, mid, qkv = call_kernel(
        spatial_forward_kernel, (ROWS_OUT, MID_OUT, QKV_OUT), "spatial_forward"
    )(starts_here, shared.reshape(-1, width), gains_spatial, full_s, counts)
    mid_tokens = exchange(mid, SEQ)

    ends = jnp.cumsum(frame_counts, axis=1)
    video_id = jnp.sum(
        (ends[:, None, :] <= jnp.arange(frames, dtype=jnp.int32)[None, :, None]).astype(jnp.int32),
        axis=2,
    )
    row_bin = place * tokens // slots
    video_row = jnp.sum((bin_ids == row_bin).astype(jnp.int32)[:, None] * video_id, axis=0)
    lab_t = video_row[:, None] * tokens + jnp.arange(tokens, dtype=jnp.int32)[None]
    both, grad_temporal = call_kernel(temporal_kernel, (BOTH_OUT, GAIN_OUT), "temporal")(
        mixed, mid_tokens, gains_temporal, full_t, lab_t.reshape(rows, 1), lab_t.reshape(1, rows)
    )
    both = exchange(both, SEQ)
    moved_grad, grad_spatial = call_kernel(
        spatial_backward_kernel, (ROWS_OUT, GAIN_OUT), "spatial_backward"
    )(both, moved, gains_spatial, full_s, counts, qkv)
    block_out = call_kernel(finish_kernel, ROWS_OUT, "finish")(mid, both, full_t)
    returned = lax.all_gather(moved_grad, "rep", axis=0, tiled=False)
    latent_grad = call_kernel(pick_kernel, ROWS_OUT, "pick")(
        starts_back, returned.reshape(-1, width)
    )
    sums = jnp.stack([grad_spatial, grad_temporal]).reshape(-1, 128)
    for axis in ("y", "z", "rep"):
        sent = sums.astype(jnp.bfloat16)
        sums = jnp.sum(spread(sent, axis).astype(jnp.float32), axis=0)
    gain_grads = sums.reshape((2,) + gains_spatial.shape)
    return (block_out.reshape(latents.shape), latent_grad.reshape(latents.shape), gain_grads)


def solution(mesh):
    rep, seq = mesh.devices.shape
    deep = Mesh(mesh.devices.reshape(rep, 8, seq // 8), ("rep", "z", "y"))
    in_specs = (
        P("rep", SEQ, None, None),
        P("rep"),
        P("rep", SEQ),
        P("rep", None),
        P(),
        P(),
        P(None, SEQ),
        P(None, SEQ),
        P(None, SEQ),
        P(None, SEQ),
        P("rep", SEQ, None, None),
    )
    out_specs = (P("rep", SEQ, None, None), P("rep", SEQ, None, None), P())
    return jax.shard_map(local, mesh=deep, in_specs=in_specs, out_specs=out_specs, check_vma=False)
```

```python
import math

import jax
import jax.numpy as jnp
from jax import lax
from jax.experimental import pallas as pl
from jax.experimental.pallas import tpu as pltpu
from jax.sharding import Mesh
from jax.sharding import PartitionSpec as P

HEADS = 8
HD = 72
INNER = HEADS * HD
SEQ = ("z", "y")
CUTS = (0, 640, 1152, 1792, 2304)
U_FROM = 1664


OVER_ROWS = (((0,), (0,)), ((), ()))
OVER_LANES = (((1,), (1,)), ((), ()))
TO_POWER = math.log2(math.e) / math.sqrt(HD)


def softmax_of(raw, allowed):
    raw = jnp.where(allowed, raw * TO_POWER, -1000000000.0)
    expo = jnp.exp2(raw - jnp.max(raw, axis=0, keepdims=True))
    return expo * (1.0 / jnp.sum(expo, axis=0, keepdims=True))


def frame_blocks(left, right):
    lane = lax.broadcasted_iota(jnp.int32, (64, 128), 1)
    halves = []
    for half in range(2):
        lanes = slice(128 * half, 128 * half + 128)
        made = lax.dot_general(
            left[:, lanes], right[:, lanes], OVER_ROWS, preferred_element_type=jnp.float32
        )
        halves.append(jnp.where(lane < 64, made[:64], made[64:]))
    return jnp.concatenate(halves, axis=1)


def spread_blocks(blocks):
    lane = lax.broadcasted_iota(jnp.int32, (64, 128), 1)
    squares = []
    for half in range(2):
        block = blocks[:, 128 * half : 128 * half + 128]
        pair = [jnp.where(lane < 64, block, 0.0), jnp.where(lane < 64, 0.0, block)]
        squares.append(jnp.concatenate(pair, axis=0).astype(jnp.bfloat16))
    return squares


def times_squares(left, squares, dims):
    made = [
        lax.dot_general(
            left[:, 128 * half : 128 * half + 128], squares[half], dims,
            preferred_element_type=jnp.float32,
        )
        for half in range(2)
    ]
    return jnp.concatenate(made, axis=1)


FORWARD_DIMS = (((1,), (0,)), ((), ()))


def normed_of(v_ref):
    wide = v_ref[...].astype(jnp.float32)
    scale = lax.rsqrt(jnp.mean(wide * wide, axis=1, keepdims=True) + 1e-06)
    return wide * scale, scale


def weight_copies(full_hbm, full_ref, sems):
    return [
        pltpu.make_async_copy(
            full_hbm.at[:, CUTS[i] : CUTS[i + 1]], full_ref.at[:, CUTS[i] : CUTS[i + 1]], sems.at[i]
        )
        for i in range(4)
    ]


def load_u(full_ref, u_ref):
    lane = lax.broadcasted_iota(jnp.int32, (72, 128), 1)
    for part in range(8):
        rows = slice(72 * part, 72 * part + 72)
        block = full_ref[144 * part : 144 * part + 144, U_FROM:].astype(jnp.float32)
        left, right = pltpu.roll(block[:72], 576, 1), block[72:]
        u_ref[rows, :512] = left[:, :512]
        u_ref[rows, 512:640] = jnp.where(lane < 64, left[:, 512:], right[:, :128])
        u_ref[rows, 640:] = right[:, 128:]


def forward(v_ref, gains_ref, full_ref, copies, allowed, q_ref, k_ref, x_ref, o_ref, w_ref):
    normed, scale = normed_of(v_ref)

    def project(which, first, past):
        copies[which].wait()
        scaled = (normed * gains_ref[which : which + 1, :]).astype(jnp.bfloat16)
        made = jnp.dot(scaled, full_ref[:, first:past], preferred_element_type=jnp.float32)
        return jnp.transpose(made.astype(jnp.bfloat16)).astype(jnp.float32)

    q_ref[...] = project(0, 0, 640)[:INNER]
    k_ref[...] = project(1, 512, 1152)[64:]
    x_ref[...] = project(2, 1152, 1792)[:INNER]
    for head in range(HEADS):
        rows = slice(HD * head, HD * head + HD)
        query = q_ref[rows, :].astype(jnp.bfloat16)
        keys = k_ref[rows, :].astype(jnp.bfloat16)
        vals = x_ref[rows, :].astype(jnp.bfloat16)
        if w_ref is None:
            weights = softmax_of(frame_blocks(keys, query), allowed)
            o_ref[rows, :] = times_squares(vals, spread_blocks(weights), FORWARD_DIMS)
        else:
            raw = lax.dot_general(keys, query, OVER_ROWS, preferred_element_type=jnp.float32)
            weights = softmax_of(raw, allowed)
            w_ref[head] = weights
            o_ref[rows, :] = jnp.dot(
                vals, weights.astype(jnp.bfloat16), preferred_element_type=jnp.float32
            )
    return jnp.transpose(o_ref[...]).astype(jnp.bfloat16)


def finish(v_ref, mixed, u_ref, out_ref):
    made = jnp.dot(mixed, u_ref[...].astype(jnp.bfloat16), preferred_element_type=jnp.float32)
    made = (v_ref[...].astype(jnp.float32) + made).astype(jnp.bfloat16)
    out_ref[...] = made.reshape(out_ref.shape)


def backward(
    g_ref, v_ref, gains_ref, full_ref, copies, allowed, grad_ref, gain_ref,
    q_ref, k_ref, x_ref, o_ref, u_ref, dq_ref, dk_ref, dx_ref, w_ref,
):
    grad = g_ref[...]
    o_ref[...] = lax.dot_general(
        u_ref[...].astype(jnp.bfloat16),
        grad,
        (((1,), (1,)), ((), ())),
        preferred_element_type=jnp.float32,
    )
    zeros = jnp.zeros((640 - INNER, dq_ref.shape[1]), jnp.float32)
    dq_ref[INNER:, :] = zeros
    dk_ref[: 640 - INNER, :] = zeros
    dx_ref[INNER:, :] = zeros
    for head in range(HEADS):
        low = HD * head
        rows = slice(low, low + HD)
        query = q_ref[rows, :].astype(jnp.bfloat16)
        keys = k_ref[rows, :].astype(jnp.bfloat16)
        vals = x_ref[rows, :].astype(jnp.bfloat16)
        d_out = o_ref[rows, :].astype(jnp.bfloat16)
        if w_ref is None:
            weights = softmax_of(frame_blocks(keys, query), allowed)
            d_weights = frame_blocks(vals, d_out)
        else:
            weights = w_ref[head]
            d_weights = lax.dot_general(
                vals, d_out, OVER_ROWS, preferred_element_type=jnp.float32
            )
        along = jnp.sum(d_weights * weights, axis=0, keepdims=True)
        d_scores = weights * ((d_weights - along) * (1.0 / math.sqrt(HD)))
        if w_ref is None:
            d_scores, weights = spread_blocks(d_scores), spread_blocks(weights)
            dq = times_squares(keys, d_scores, FORWARD_DIMS)
            dk = times_squares(query, d_scores, OVER_LANES)
            dx = times_squares(d_out, weights, OVER_LANES)
        else:
            d_scores, weights = d_scores.astype(jnp.bfloat16), weights.astype(jnp.bfloat16)
            dq = jnp.dot(keys, d_scores, preferred_element_type=jnp.float32)
            dk = lax.dot_general(query, d_scores, OVER_LANES, preferred_element_type=jnp.float32)
            dx = lax.dot_general(d_out, weights, OVER_LANES, preferred_element_type=jnp.float32)
        dq_ref[rows, :] = dq
        dk_ref[64 + low : 64 + low + HD, :] = dk
        dx_ref[rows, :] = dx
    normed, scale = normed_of(v_ref)
    for copy in copies:
        copy.wait()
    d_normed = None
    for which, (ref, first) in enumerate(((dq_ref, 0), (dk_ref, 512), (dx_ref, 1152))):
        made = jnp.transpose(ref[...]).astype(jnp.bfloat16)
        back = lax.dot_general(
            made, full_ref[:, first : first + 640], OVER_LANES, preferred_element_type=jnp.float32
        )
        gain_ref[which : which + 1, :] = jnp.sum(back * normed, axis=0, keepdims=True)
        term = back * gains_ref[which : which + 1, :]
        d_normed = term if d_normed is None else d_normed + term
    inward = jnp.mean(d_normed * normed, axis=1, keepdims=True)
    result = grad.astype(jnp.float32) + scale * (d_normed - normed * inward)
    grad_ref[...] = result.astype(jnp.bfloat16)


def valid_keys(counts):
    return lax.broadcasted_iota(jnp.int32, (64, 256), 0) < counts[...]


def spatial_forward_kernel(
    starts, everyone, gains, full_hbm, counts, moved, mid, qkv,
    full, sems, u, q, k, x, o, pick_sems,
):
    copies = weight_copies(full_hbm, full, sems)
    picks = [
        pltpu.make_async_copy(
            everyone.at[pl.ds(pl.multiple_of(starts[i], 16), 64), :],
            moved.at[64 * i : 64 * i + 64, :],
            pick_sems.at[i],
        )
        for i in range(4)
    ]
    for copy in picks + copies[:1]:
        copy.start()
    for copy in picks:
        copy.wait()
    for copy in copies[1:]:
        copy.start()
    mixed = forward(moved, gains, full, copies, valid_keys(counts), q, k, x, o, None)
    copies[3].wait()
    load_u(full, u)
    finish(moved, mixed, u, mid)
    for which, ref in enumerate((q, k, x)):
        qkv[which] = ref[...].astype(jnp.bfloat16)


def spatial_backward_kernel(
    both, v, gains, full_hbm, counts, qkv, grad, gain,
    full, sems, u, q, k, x, o, dq, dk, dx, g,
):
    copies = weight_copies(full_hbm, full, sems)
    for copy in copies[::-1]:
        copy.start()
    for which, ref in enumerate((q, k, x)):
        ref[...] = qkv[which].astype(jnp.float32)
    g[...] = both[:, :, :1152].reshape(g.shape)
    copies[3].wait()
    copies[2].wait()
    load_u(full, u)
    backward(
        g, v, gains, full, copies[:2], valid_keys(counts), grad, gain,
        q, k, x, o, u, dq, dk, dx, None,
    )


def temporal_kernel(
    got, mid, gains, full_hbm, lab_k, lab_q, both, gain,
    full, sems, u, q, k, x, o, dq, dk, dx, g, v, grad, w,
):
    copies = weight_copies(full_hbm, full, sems)
    for copy in copies:
        copy.start()
    v[...] = mid[...].reshape(v.shape)
    g[...] = got[:, :, :1152].reshape(g.shape)
    allowed = lab_k[...] == lab_q[...]
    mixed = forward(v, gains, full, copies, allowed, q, k, x, o, w)
    both[:, :, 1152:] = mixed.reshape(both.shape[0], both.shape[1], INNER)
    copies[3].wait()
    load_u(full, u)
    backward(
        g, v, gains, full, [], allowed, grad, gain, q, k, x, o, u, dq, dk, dx, w
    )
    both[:, :, :1152] = grad[...].reshape(both.shape[0], both.shape[1], 1152)


def finish_kernel(mid, both, full_hbm, out, full, sems, u, v):
    copies = weight_copies(full_hbm, full, sems)[2:]
    for copy in copies:
        copy.start()
    v[...] = mid[...].reshape(v.shape)
    mixed = both[:, :, 1152:].reshape(v.shape[0], INNER)
    for copy in copies:
        copy.wait()
    load_u(full, u)
    finish(v, mixed, u, out)


def pick_kernel(starts, everyone, out, sems):
    picks = [
        pltpu.make_async_copy(
            everyone.at[pl.ds(pl.multiple_of(starts[i], 16), 64), :],
            out.at[64 * i : 64 * i + 64, :],
            sems.at[i],
        )
        for i in range(4)
    ]
    for copy in picks:
        copy.start()
    for copy in picks:
        copy.wait()


def call_kernel(kernel, outs, name):
    vmem = pl.BlockSpec(memory_space=pltpu.VMEM)
    smem = pl.BlockSpec(memory_space=pltpu.SMEM)
    hbm = pl.BlockSpec(memory_space=pl.ANY)
    rows = 256
    four = pltpu.SemaphoreType.DMA((4,))
    scratch = [
        pltpu.VMEM((1152, CUTS[-1]), jnp.bfloat16), four, pltpu.VMEM((INNER, 1152), jnp.float32)
    ]
    scratch += [pltpu.VMEM((INNER, rows), jnp.float32)] * 4
    flat = pltpu.VMEM((rows, 1152), jnp.bfloat16)
    backs = [pltpu.VMEM((640, rows), jnp.float32)] * 3
    if kernel is finish_kernel:
        ins, scratch = [vmem, vmem, hbm], scratch[:3] + [flat]
    elif kernel is pick_kernel:
        ins, scratch = [smem, hbm], [four]
    elif kernel is spatial_forward_kernel:
        ins, scratch = [smem, hbm, vmem, hbm, vmem], scratch + [four]
    elif kernel is temporal_kernel:
        ins, scratch = [vmem] * 3 + [hbm] + [vmem] * 2, scratch + backs + [flat] * 3
        scratch = scratch + [pltpu.VMEM((HEADS, rows, rows), jnp.float32)]
    else:
        ins, scratch = [vmem] * 3 + [hbm] + [vmem] * 2, scratch + backs + [flat]
    return pl.pallas_call(
        kernel,
        out_shape=outs,
        in_specs=ins,
        out_specs=jax.tree.map(lambda _: vmem, outs),
        scratch_shapes=scratch,
        compiler_params=pltpu.CompilerParams(vmem_limit_bytes=50 * 1024 * 1024),
        cost_estimate=pl.CostEstimate(
            flops=int(6e9), bytes_accessed=int(8e6), transcendentals=int(5e5)
        ),
        name=name,
    )


ROWS_OUT = jax.ShapeDtypeStruct((256, 1152), jnp.bfloat16)
MID_OUT = jax.ShapeDtypeStruct((64, 4, 1152), jnp.bfloat16)
BOTH_OUT = jax.ShapeDtypeStruct((64, 4, 1728), jnp.bfloat16)
GAIN_OUT = jax.ShapeDtypeStruct((3, 1152), jnp.float32)
QKV_OUT = jax.ShapeDtypeStruct((3, 576, 256), jnp.bfloat16)


def exchange(rows, axes):
    return lax.all_to_all(rows, axes, split_axis=0, concat_axis=0, tiled=True)


def spread(value, axes):
    peers = lax.axis_size(axes)
    return exchange(jnp.broadcast_to(value[None], (peers,) + value.shape), axes)


def own_piece(qkv, proj, rep, groups):
    rows_w, rows_u = qkv.shape[0] // groups, proj.shape[0] // groups
    piece_w = lax.dynamic_slice(qkv.T, (0, rep * rows_w), (qkv.shape[1], rows_w)).reshape(-1)
    piece_u = lax.dynamic_slice(proj.T, (0, rep * rows_u), (proj.shape[1], rows_u)).reshape(-1)
    return jnp.concatenate([piece_w, piece_u])


def gather_weights(got, shard, shard_u, rows_w, rows_u):
    peers = got.shape[0]
    cut = shard * rows_w
    part_w = got[:, :cut].reshape(peers * shard, rows_w).T
    part_u = got[:, cut : cut + shard_u * rows_u].reshape(peers * shard_u, rows_u).T
    half = part_u.shape[1] // 2
    part_u = jnp.concatenate([part_u[:, :half], part_u[:, half:]], axis=0)
    part = jnp.concatenate([part_w, part_u], axis=1)
    full = lax.all_gather(part, "rep", axis=0, tiled=False)
    return full.reshape(full.shape[0] * full.shape[1], full.shape[2])


def local(
    latents,
    destination,
    token_counts,
    frame_counts,
    gains_spatial,
    gains_temporal,
    qkv_spatial,
    proj_spatial,
    qkv_temporal,
    proj_temporal,
    cotangent,
):
    bins_here, _, slots, width = latents.shape
    groups = lax.axis_size("rep")
    frames = lax.axis_size(SEQ)
    group = lax.axis_index("rep")
    place = lax.axis_index(SEQ)
    inner = proj_spatial.shape[0]
    tokens = bins_here * slots // frames
    rows = bins_here * slots
    sizes = (qkv_spatial.shape[1], proj_spatial.shape[1], width // groups, inner // groups)

    mine = jnp.pad(destination.astype(jnp.bfloat16)[None], ((0, 15), (0, width - bins_here)))
    sent = jnp.concatenate([latents.reshape(rows, width), mine], axis=0)
    shared = lax.all_gather(sent, "rep", axis=0, tiled=False)

    flat_s = own_piece(qkv_spatial, proj_spatial, group, groups)
    flat_s = jnp.pad(flat_s, (0, -flat_s.shape[0] % 256))
    got_s = spread(flat_s.reshape(2, -1), SEQ)

    flat_t = own_piece(qkv_temporal, proj_temporal, group, groups).reshape(tokens, -1)
    flat_t = jnp.pad(flat_t, ((0, 0), (0, -flat_t.shape[1] % 128)))
    mixed = jnp.concatenate(
        [
            cotangent.reshape(frames, tokens, width),
            jnp.broadcast_to(flat_t[None], (frames,) + flat_t.shape),
        ],
        axis=2,
    )
    got_s, mixed = lax.optimization_barrier((got_s, mixed))
    full_s = gather_weights(got_s.reshape(frames, -1), *sizes)
    mixed = exchange(mixed, SEQ)
    piece = sizes[0] * sizes[2] + sizes[1] * sizes[3]
    full_t = gather_weights(
        mixed[:, :, width : width + piece // tokens].reshape(frames, -1), *sizes
    )

    dest_all = shared[:, rows, :bins_here].astype(jnp.int32)
    group_ids = jnp.arange(groups, dtype=jnp.int32)
    bin_ids = jnp.arange(bins_here, dtype=jnp.int32)
    here = (dest_all == group).astype(jnp.int32)
    comes = jnp.sum(here, axis=1)
    order = jnp.sum((group_ids[None] < group_ids[:, None]).astype(jnp.int32) * comes[None], axis=1)
    source = (order[None] == bin_ids[:, None]).astype(jnp.int32) * comes[None]
    from_group = jnp.sum(source * group_ids[None], axis=1)
    from_bin = jnp.sum(source * jnp.sum(here * bin_ids[None], axis=1)[None], axis=1)
    earlier = (dest_all[None] == destination[:, None, None]) & (group_ids[None, :, None] < group)
    rank = jnp.sum(earlier.astype(jnp.int32), axis=(1, 2))

    starts_here = from_group * shared.shape[1] + from_bin * slots
    starts_back = destination * rows + rank * slots
    counts = jnp.broadcast_to(token_counts, (bins_here, slots)).reshape(1, rows)
    moved, mid, qkv = call_kernel(
        spatial_forward_kernel, (ROWS_OUT, MID_OUT, QKV_OUT), "spatial_forward"
    )(starts_here, shared.reshape(-1, width), gains_spatial, full_s, counts)
    mid_tokens = exchange(mid, SEQ)

    ends = jnp.cumsum(frame_counts, axis=1)
    video_id = jnp.sum(
        (ends[:, None, :] <= jnp.arange(frames, dtype=jnp.int32)[None, :, None]).astype(jnp.int32),
        axis=2,
    )
    row_bin = place * tokens // slots
    video_row = jnp.sum((bin_ids == row_bin).astype(jnp.int32)[:, None] * video_id, axis=0)
    lab_t = video_row[:, None] * tokens + jnp.arange(tokens, dtype=jnp.int32)[None]
    both, grad_temporal = call_kernel(temporal_kernel, (BOTH_OUT, GAIN_OUT), "temporal")(
        mixed, mid_tokens, gains_temporal, full_t, lab_t.reshape(rows, 1), lab_t.reshape(1, rows)
    )
    both = exchange(both, SEQ)
    moved_grad, grad_spatial = call_kernel(
        spatial_backward_kernel, (ROWS_OUT, GAIN_OUT), "spatial_backward"
    )(both, moved, gains_spatial, full_s, counts, qkv)
    block_out = call_kernel(finish_kernel, ROWS_OUT, "finish")(mid, both, full_t)
    returned = lax.all_gather(moved_grad, "rep", axis=0, tiled=False)
    latent_grad = call_kernel(pick_kernel, ROWS_OUT, "pick")(
        starts_back, returned.reshape(-1, width)
    )
    sums = jnp.stack([grad_spatial, grad_temporal]).reshape(-1, 128)
    for axis in ("y", "z", "rep"):
        got = spread(sums.astype(jnp.bfloat16), axis)
        if axis == "y":
            got, block_out = lax.optimization_barrier((got, block_out))
        if axis == "rep":
            got, latent_grad = lax.optimization_barrier((got, latent_grad))
        sums = jnp.sum(got.astype(jnp.float32), axis=0)
    gain_grads = sums.reshape((2,) + gains_spatial.shape)
    return (block_out.reshape(latents.shape), latent_grad.reshape(latents.shape), gain_grads)


def solution(mesh):
    rep, seq = mesh.devices.shape
    deep = Mesh(mesh.devices.reshape(rep, 8, seq // 8), ("rep", "z", "y"))
    in_specs = (
        P("rep", SEQ, None, None),
        P("rep"),
        P("rep", SEQ),
        P("rep", None),
        P(),
        P(),
        P(None, SEQ),
        P(None, SEQ),
        P(None, SEQ),
        P(None, SEQ),
        P("rep", SEQ, None, None),
    )
    out_specs = (P("rep", SEQ, None, None), P("rep", SEQ, None, None), P())
    return jax.shard_map(local, mesh=deep, in_specs=in_specs, out_specs=out_specs, check_vma=False)
```

```python
import math

import jax
import jax.numpy as jnp
from jax import lax
from jax.experimental import pallas as pl
from jax.experimental.pallas import tpu as pltpu
from jax.sharding import Mesh
from jax.sharding import PartitionSpec as P

HEADS = 8
HD = 72
INNER = HEADS * HD
SEQ = ("z", "y")
CUTS = (0, 640, 1152, 1792, 2304)
U_FROM = 1664


OVER_ROWS = (((0,), (0,)), ((), ()))
OVER_LANES = (((1,), (1,)), ((), ()))
TO_POWER = math.log2(math.e) / math.sqrt(HD)


def softmax_of(raw, allowed):
    raw = jnp.where(allowed, raw * TO_POWER, -1000000000.0)
    expo = jnp.exp2(raw - jnp.max(raw, axis=0, keepdims=True))
    return expo * (1.0 / jnp.sum(expo, axis=0, keepdims=True))


def frame_blocks(left, right):
    lane = lax.broadcasted_iota(jnp.int32, (64, 128), 1)
    halves = []
    for half in range(2):
        lanes = slice(128 * half, 128 * half + 128)
        made = lax.dot_general(
            left[:, lanes], right[:, lanes], OVER_ROWS, preferred_element_type=jnp.float32
        )
        halves.append(jnp.where(lane < 64, made[:64], made[64:]))
    return jnp.concatenate(halves, axis=1)


def spread_blocks(blocks):
    lane = lax.broadcasted_iota(jnp.int32, (64, 128), 1)
    squares = []
    for half in range(2):
        block = blocks[:, 128 * half : 128 * half + 128]
        pair = [jnp.where(lane < 64, block, 0.0), jnp.where(lane < 64, 0.0, block)]
        squares.append(jnp.concatenate(pair, axis=0).astype(jnp.bfloat16))
    return squares


def times_squares(left, squares, dims):
    made = [
        lax.dot_general(
            left[:, 128 * half : 128 * half + 128], squares[half], dims,
            preferred_element_type=jnp.float32,
        )
        for half in range(2)
    ]
    return jnp.concatenate(made, axis=1)


FORWARD_DIMS = (((1,), (0,)), ((), ()))


def normed_of(v_ref):
    wide = v_ref[...].astype(jnp.float32)
    scale = lax.rsqrt(jnp.mean(wide * wide, axis=1, keepdims=True) + 1e-06)
    return wide * scale, scale


def weight_copies(full_hbm, full_ref, sems):
    return [
        pltpu.make_async_copy(
            full_hbm.at[:, CUTS[i] : CUTS[i + 1]], full_ref.at[:, CUTS[i] : CUTS[i + 1]], sems.at[i]
        )
        for i in range(4)
    ]


def load_u(full_ref, u_ref):
    lane = lax.broadcasted_iota(jnp.int32, (72, 128), 1)
    for part in range(8):
        rows = slice(72 * part, 72 * part + 72)
        block = full_ref[144 * part : 144 * part + 144, U_FROM:].astype(jnp.float32)
        left, right = pltpu.roll(block[:72], 576, 1), block[72:]
        u_ref[rows, :512] = left[:, :512]
        u_ref[rows, 512:640] = jnp.where(lane < 64, left[:, 512:], right[:, :128])
        u_ref[rows, 640:] = right[:, 128:]


def forward(v_ref, gains_ref, full_ref, copies, allowed, q_ref, k_ref, x_ref, o_ref, w_ref):
    normed, scale = normed_of(v_ref)

    def project(which, first, past):
        copies[which].wait()
        scaled = (normed * gains_ref[which : which + 1, :]).astype(jnp.bfloat16)
        made = jnp.dot(scaled, full_ref[:, first:past], preferred_element_type=jnp.float32)
        return jnp.transpose(made.astype(jnp.bfloat16)).astype(jnp.float32)

    q_ref[...] = project(0, 0, 640)[:INNER]
    k_ref[...] = project(1, 512, 1152)[64:]
    x_ref[...] = project(2, 1152, 1792)[:INNER]
    for head in range(HEADS):
        rows = slice(HD * head, HD * head + HD)
        query = q_ref[rows, :].astype(jnp.bfloat16)
        keys = k_ref[rows, :].astype(jnp.bfloat16)
        vals = x_ref[rows, :].astype(jnp.bfloat16)
        if w_ref is None:
            weights = softmax_of(frame_blocks(keys, query), allowed)
            o_ref[rows, :] = times_squares(vals, spread_blocks(weights), FORWARD_DIMS)
        else:
            raw = lax.dot_general(keys, query, OVER_ROWS, preferred_element_type=jnp.float32)
            weights = softmax_of(raw, allowed)
            w_ref[head] = weights
            o_ref[rows, :] = jnp.dot(
                vals, weights.astype(jnp.bfloat16), preferred_element_type=jnp.float32
            )
    return jnp.transpose(o_ref[...]).astype(jnp.bfloat16)


def finish(v_ref, mixed, u_ref, out_ref):
    made = jnp.dot(mixed, u_ref[...].astype(jnp.bfloat16), preferred_element_type=jnp.float32)
    made = (v_ref[...].astype(jnp.float32) + made).astype(jnp.bfloat16)
    out_ref[...] = made.reshape(out_ref.shape)


def backward(
    g_ref, v_ref, gains_ref, full_ref, copies, allowed, grad_ref, gain_ref,
    q_ref, k_ref, x_ref, o_ref, u_ref, dq_ref, dk_ref, dx_ref, w_ref,
):
    grad = g_ref[...]
    o_ref[...] = lax.dot_general(
        u_ref[...].astype(jnp.bfloat16),
        grad,
        (((1,), (1,)), ((), ())),
        preferred_element_type=jnp.float32,
    )
    zeros = jnp.zeros((640 - INNER, dq_ref.shape[1]), jnp.float32)
    dq_ref[INNER:, :] = zeros
    dk_ref[: 640 - INNER, :] = zeros
    dx_ref[INNER:, :] = zeros
    for head in range(HEADS):
        low = HD * head
        rows = slice(low, low + HD)
        query = q_ref[rows, :].astype(jnp.bfloat16)
        keys = k_ref[rows, :].astype(jnp.bfloat16)
        vals = x_ref[rows, :].astype(jnp.bfloat16)
        d_out = o_ref[rows, :].astype(jnp.bfloat16)
        if w_ref is None:
            weights = softmax_of(frame_blocks(keys, query), allowed)
            d_weights = frame_blocks(vals, d_out)
        else:
            weights = w_ref[head]
            d_weights = lax.dot_general(
                vals, d_out, OVER_ROWS, preferred_element_type=jnp.float32
            )
        along = jnp.sum(d_weights * weights, axis=0, keepdims=True)
        d_scores = weights * ((d_weights - along) * (1.0 / math.sqrt(HD)))
        if w_ref is None:
            d_scores, weights = spread_blocks(d_scores), spread_blocks(weights)
            dq = times_squares(keys, d_scores, FORWARD_DIMS)
            dk = times_squares(query, d_scores, OVER_LANES)
            dx = times_squares(d_out, weights, OVER_LANES)
        else:
            d_scores, weights = d_scores.astype(jnp.bfloat16), weights.astype(jnp.bfloat16)
            dq = jnp.dot(keys, d_scores, preferred_element_type=jnp.float32)
            dk = lax.dot_general(query, d_scores, OVER_LANES, preferred_element_type=jnp.float32)
            dx = lax.dot_general(d_out, weights, OVER_LANES, preferred_element_type=jnp.float32)
        dq_ref[rows, :] = dq
        dk_ref[64 + low : 64 + low + HD, :] = dk
        dx_ref[rows, :] = dx
    normed, scale = normed_of(v_ref)
    for copy in copies:
        copy.wait()
    d_normed = None
    for which, (ref, first) in enumerate(((dq_ref, 0), (dk_ref, 512), (dx_ref, 1152))):
        made = jnp.transpose(ref[...]).astype(jnp.bfloat16)
        back = lax.dot_general(
            made, full_ref[:, first : first + 640], OVER_LANES, preferred_element_type=jnp.float32
        )
        gain_ref[which : which + 1, :] = jnp.sum(back * normed, axis=0, keepdims=True)
        term = back * gains_ref[which : which + 1, :]
        d_normed = term if d_normed is None else d_normed + term
    inward = jnp.mean(d_normed * normed, axis=1, keepdims=True)
    result = grad.astype(jnp.float32) + scale * (d_normed - normed * inward)
    grad_ref[...] = result.astype(jnp.bfloat16)


def valid_keys(counts):
    return lax.broadcasted_iota(jnp.int32, (64, 256), 0) < counts[...]


def spatial_forward_kernel(
    starts, everyone, gains, full_hbm, counts, moved, mid, qkv,
    full, sems, u, q, k, x, o, pick_sems,
):
    copies = weight_copies(full_hbm, full, sems)
    picks = [
        pltpu.make_async_copy(
            everyone.at[pl.ds(pl.multiple_of(starts[i], 16), 64), :],
            moved.at[64 * i : 64 * i + 64, :],
            pick_sems.at[i],
        )
        for i in range(4)
    ]
    for copy in picks + copies[:1]:
        copy.start()
    for copy in picks:
        copy.wait()
    for copy in copies[1:]:
        copy.start()
    mixed = forward(moved, gains, full, copies, valid_keys(counts), q, k, x, o, None)
    copies[3].wait()
    load_u(full, u)
    finish(moved, mixed, u, mid)
    for which, ref in enumerate((q, k, x)):
        qkv[which] = ref[...].astype(jnp.bfloat16)


def spatial_backward_kernel(
    both, v, gains, full_hbm, counts, qkv, grad, gain,
    full, sems, u, q, k, x, o, dq, dk, dx, g,
):
    copies = weight_copies(full_hbm, full, sems)
    for copy in copies[2:]:
        copy.start()
    for which, ref in enumerate((q, k, x)):
        ref[...] = qkv[which].astype(jnp.float32)
    g[...] = both[:, :, :1152].reshape(g.shape)
    for copy in copies[2:]:
        copy.wait()
    for copy in copies[:2]:
        copy.start()
    load_u(full, u)
    backward(
        g, v, gains, full, copies[:2], valid_keys(counts), grad, gain,
        q, k, x, o, u, dq, dk, dx, None,
    )


def temporal_kernel(
    got, mid, gains, full_hbm, lab_k, lab_q, both, gain,
    full, sems, u, q, k, x, o, dq, dk, dx, g, v, grad, w,
):
    copies = weight_copies(full_hbm, full, sems)
    for copy in copies:
        copy.start()
    v[...] = mid[...].reshape(v.shape)
    g[...] = got[:, :, :1152].reshape(g.shape)
    allowed = lab_k[...] == lab_q[...]
    mixed = forward(v, gains, full, copies, allowed, q, k, x, o, w)
    both[:, :, 1152:] = mixed.reshape(both.shape[0], both.shape[1], INNER)
    copies[3].wait()
    load_u(full, u)
    backward(
        g, v, gains, full, [], allowed, grad, gain, q, k, x, o, u, dq, dk, dx, w
    )
    both[:, :, :1152] = grad[...].reshape(both.shape[0], both.shape[1], 1152)


def finish_kernel(mid, both, full_hbm, out, full, sems, u, v):
    copies = weight_copies(full_hbm, full, sems)[2:]
    for copy in copies:
        copy.start()
    v[...] = mid[...].reshape(v.shape)
    mixed = both[:, :, 1152:].reshape(v.shape[0], INNER)
    for copy in copies:
        copy.wait()
    load_u(full, u)
    finish(v, mixed, u, out)


def pick_kernel(starts, everyone, out, sems):
    picks = [
        pltpu.make_async_copy(
            everyone.at[pl.ds(pl.multiple_of(starts[i], 16), 64), :],
            out.at[64 * i : 64 * i + 64, :],
            sems.at[i],
        )
        for i in range(4)
    ]
    for copy in picks:
        copy.start()
    for copy in picks:
        copy.wait()


def call_kernel(kernel, outs, name):
    vmem = pl.BlockSpec(memory_space=pltpu.VMEM)
    smem = pl.BlockSpec(memory_space=pltpu.SMEM)
    hbm = pl.BlockSpec(memory_space=pl.ANY)
    rows = 256
    four = pltpu.SemaphoreType.DMA((4,))
    scratch = [
        pltpu.VMEM((1152, CUTS[-1]), jnp.bfloat16), four, pltpu.VMEM((INNER, 1152), jnp.float32)
    ]
    scratch += [pltpu.VMEM((INNER, rows), jnp.float32)] * 4
    flat = pltpu.VMEM((rows, 1152), jnp.bfloat16)
    backs = [pltpu.VMEM((640, rows), jnp.float32)] * 3
    if kernel is finish_kernel:
        ins, scratch = [vmem, vmem, hbm], scratch[:3] + [flat]
    elif kernel is pick_kernel:
        ins, scratch = [smem, hbm], [four]
    elif kernel is spatial_forward_kernel:
        ins, scratch = [smem, hbm, vmem, hbm, vmem], scratch + [four]
    elif kernel is temporal_kernel:
        ins, scratch = [vmem] * 3 + [hbm] + [vmem] * 2, scratch + backs + [flat] * 3
        scratch = scratch + [pltpu.VMEM((HEADS, rows, rows), jnp.float32)]
    else:
        ins, scratch = [vmem] * 3 + [hbm] + [vmem] * 2, scratch + backs + [flat]
    return pl.pallas_call(
        kernel,
        out_shape=outs,
        in_specs=ins,
        out_specs=jax.tree.map(lambda _: vmem, outs),
        scratch_shapes=scratch,
        compiler_params=pltpu.CompilerParams(vmem_limit_bytes=50 * 1024 * 1024),
        cost_estimate=pl.CostEstimate(
            flops=int(6e9), bytes_accessed=int(8e6), transcendentals=int(5e5)
        ),
        name=name,
    )


ROWS_OUT = jax.ShapeDtypeStruct((256, 1152), jnp.bfloat16)
MID_OUT = jax.ShapeDtypeStruct((64, 4, 1152), jnp.bfloat16)
BOTH_OUT = jax.ShapeDtypeStruct((64, 4, 1728), jnp.bfloat16)
GAIN_OUT = jax.ShapeDtypeStruct((3, 1152), jnp.float32)
QKV_OUT = jax.ShapeDtypeStruct((3, 576, 256), jnp.bfloat16)


def exchange(rows, axes):
    return lax.all_to_all(rows, axes, split_axis=0, concat_axis=0, tiled=True)


def spread(value, axes):
    peers = lax.axis_size(axes)
    return exchange(jnp.broadcast_to(value[None], (peers,) + value.shape), axes)


def own_piece(qkv, proj, rep, groups):
    rows_w, rows_u = qkv.shape[0] // groups, proj.shape[0] // groups
    piece_w = lax.dynamic_slice(qkv.T, (0, rep * rows_w), (qkv.shape[1], rows_w)).reshape(-1)
    piece_u = lax.dynamic_slice(proj.T, (0, rep * rows_u), (proj.shape[1], rows_u)).reshape(-1)
    return jnp.concatenate([piece_w, piece_u])


def gather_weights(got, shard, shard_u, rows_w, rows_u):
    peers = got.shape[0]
    cut = shard * rows_w
    part_w = got[:, :cut].reshape(peers * shard, rows_w).T
    part_u = got[:, cut : cut + shard_u * rows_u].reshape(peers * shard_u, rows_u).T
    half = part_u.shape[1] // 2
    part_u = jnp.concatenate([part_u[:, :half], part_u[:, half:]], axis=0)
    part = jnp.concatenate([part_w, part_u], axis=1)
    full = lax.all_gather(part, "rep", axis=0, tiled=False)
    return full.reshape(full.shape[0] * full.shape[1], full.shape[2])


def local(
    latents,
    destination,
    token_counts,
    frame_counts,
    gains_spatial,
    gains_temporal,
    qkv_spatial,
    proj_spatial,
    qkv_temporal,
    proj_temporal,
    cotangent,
):
    bins_here, _, slots, width = latents.shape
    groups = lax.axis_size("rep")
    frames = lax.axis_size(SEQ)
    group = lax.axis_index("rep")
    place = lax.axis_index(SEQ)
    inner = proj_spatial.shape[0]
    tokens = bins_here * slots // frames
    rows = bins_here * slots
    sizes = (qkv_spatial.shape[1], proj_spatial.shape[1], width // groups, inner // groups)

    mine = jnp.pad(destination.astype(jnp.bfloat16)[None], ((0, 15), (0, width - bins_here)))
    sent = jnp.concatenate([latents.reshape(rows, width), mine], axis=0)
    shared = lax.all_gather(sent, "rep", axis=0, tiled=False)

    flat_s = own_piece(qkv_spatial, proj_spatial, group, groups)
    flat_s = jnp.pad(flat_s, (0, -flat_s.shape[0] % 256))
    got_s = spread(flat_s.reshape(2, -1), SEQ)

    flat_t = own_piece(qkv_temporal, proj_temporal, group, groups).reshape(tokens, -1)
    flat_t = jnp.pad(flat_t, ((0, 0), (0, -flat_t.shape[1] % 128)))
    mixed = jnp.concatenate(
        [
            cotangent.reshape(frames, tokens, width),
            jnp.broadcast_to(flat_t[None], (frames,) + flat_t.shape),
        ],
        axis=2,
    )
    got_s, mixed = lax.optimization_barrier((got_s, mixed))
    full_s = gather_weights(got_s.reshape(frames, -1), *sizes)
    mixed = exchange(mixed, SEQ)
    piece = sizes[0] * sizes[2] + sizes[1] * sizes[3]
    full_t = gather_weights(
        mixed[:, :, width : width + piece // tokens].reshape(frames, -1), *sizes
    )

    dest_all = shared[:, rows, :bins_here].astype(jnp.int32)
    group_ids = jnp.arange(groups, dtype=jnp.int32)
    bin_ids = jnp.arange(bins_here, dtype=jnp.int32)
    here = (dest_all == group).astype(jnp.int32)
    comes = jnp.sum(here, axis=1)
    order = jnp.sum((group_ids[None] < group_ids[:, None]).astype(jnp.int32) * comes[None], axis=1)
    source = (order[None] == bin_ids[:, None]).astype(jnp.int32) * comes[None]
    from_group = jnp.sum(source * group_ids[None], axis=1)
    from_bin = jnp.sum(source * jnp.sum(here * bin_ids[None], axis=1)[None], axis=1)
    earlier = (dest_all[None] == destination[:, None, None]) & (group_ids[None, :, None] < group)
    rank = jnp.sum(earlier.astype(jnp.int32), axis=(1, 2))

    starts_here = from_group * shared.shape[1] + from_bin * slots
    starts_back = destination * rows + rank * slots
    counts = jnp.broadcast_to(token_counts, (bins_here, slots)).reshape(1, rows)
    moved, mid, qkv = call_kernel(
        spatial_forward_kernel, (ROWS_OUT, MID_OUT, QKV_OUT), "spatial_forward"
    )(starts_here, shared.reshape(-1, width), gains_spatial, full_s, counts)
    mid_tokens = exchange(mid, SEQ)

    ends = jnp.cumsum(frame_counts, axis=1)
    video_id = jnp.sum(
        (ends[:, None, :] <= jnp.arange(frames, dtype=jnp.int32)[None, :, None]).astype(jnp.int32),
        axis=2,
    )
    row_bin = place * tokens // slots
    video_row = jnp.sum((bin_ids == row_bin).astype(jnp.int32)[:, None] * video_id, axis=0)
    lab_t = video_row[:, None] * tokens + jnp.arange(tokens, dtype=jnp.int32)[None]
    both, grad_temporal = call_kernel(temporal_kernel, (BOTH_OUT, GAIN_OUT), "temporal")(
        mixed, mid_tokens, gains_temporal, full_t, lab_t.reshape(rows, 1), lab_t.reshape(1, rows)
    )
    both = exchange(both, SEQ)
    moved_grad, grad_spatial = call_kernel(
        spatial_backward_kernel, (ROWS_OUT, GAIN_OUT), "spatial_backward"
    )(both, moved, gains_spatial, full_s, counts, qkv)
    block_out = call_kernel(finish_kernel, ROWS_OUT, "finish")(mid, both, full_t)
    returned = lax.all_gather(moved_grad, "rep", axis=0, tiled=False)
    latent_grad = call_kernel(pick_kernel, ROWS_OUT, "pick")(
        starts_back, returned.reshape(-1, width)
    )
    sums = jnp.stack([grad_spatial, grad_temporal]).reshape(-1, 128)
    for axis in ("y", "z", "rep"):
        got = spread(sums.astype(jnp.bfloat16), axis)
        if axis == "y":
            got, block_out = lax.optimization_barrier((got, block_out))
        if axis == "rep":
            got, latent_grad = lax.optimization_barrier((got, latent_grad))
        sums = jnp.sum(got.astype(jnp.float32), axis=0)
    gain_grads = sums.reshape((2,) + gains_spatial.shape)
    return (block_out.reshape(latents.shape), latent_grad.reshape(latents.shape), gain_grads)


def solution(mesh):
    rep, seq = mesh.devices.shape
    deep = Mesh(mesh.devices.reshape(rep, 8, seq // 8), ("rep", "z", "y"))
    in_specs = (
        P("rep", SEQ, None, None),
        P("rep"),
        P("rep", SEQ),
        P("rep", None),
        P(),
        P(),
        P(None, SEQ),
        P(None, SEQ),
        P(None, SEQ),
        P(None, SEQ),
        P("rep", SEQ, None, None),
    )
    out_specs = (P("rep", SEQ, None, None), P("rep", SEQ, None, None), P())
    return jax.shard_map(local, mesh=deep, in_specs=in_specs, out_specs=out_specs, check_vma=False)
```
